32 devices in a mesh: tm: 4 (over z), dof: 8 (over y, x, core).
Axes of the slice: x: 2, y: 2, z: 4, core: 2. Of those that a mesh axis runs over, the one named last changes fastest.
Arguments:
- loads: bfloat16 [1536, 4096], P('tm', 'dof'), may hold values from -6 to 6
- phi: bfloat16 [6144, 4096], P('dof'), may hold values from -0.125 to 0.125
- load_index: int32 [4096], P('dof'), may hold values from 0 to 6143, as said below
- damping: float32 [4096], P('dof'), may hold values from 0.00013020834 to 0.05
- frequency: float32 [4096], P('dof'), may hold values from 0.05 to 1.5
- gains: float32 [1536], P('tm'), may hold values from 0.25 to 1
- shapes: bfloat16 [4096, 16384], P(None, 'dof'), may hold values from -0.09375 to 0.09375
Outputs:
- field: bfloat16 [1536, 16384], P('tm', 'dof')
- history: float32 [4096, 1536], P('dof', 'tm')
The draws below stay inside these ranges and needn't reach their ends.
Inputs may be any that keep to these rules, and one draw needn't show every extreme that they name: `load_index`: entries k * 512 to (k + 1) * 512 - 1 name rows k * 768 to (k + 1) * 768 - 1; rows may repeat.
All inputs are finite; a program needn't handle non-finite values.
Results may differ from the reference program's by a relative error of at most 0.0049.
Values may be sent and summed in bfloat16 or wider, within the bound.
A program may use at most 128 MiB of HBM per device.

```python
import math
import jax
import jax.numpy as jnp
from jax import lax

M = 4096
LOAD_DEV = 512
DOF_DEV = 768
TIMES = 1536
LOADS = 4096
NDOF = 6144
NFP = 16384


def draw_load_index(key, part):
    places = jnp.arange(LOADS, dtype=jnp.int32)
    slot = places % LOAD_DEV
    local = jax.random.randint(key, (LOADS,), 0, DOF_DEV, dtype=jnp.int32)
    local = jnp.where(slot == 0, 0, jnp.where(slot == 1, DOF_DEV - 1, local))
    return places // LOAD_DEV * DOF_DEV + local


def draw_gains(key, part):
    first, second, third = jax.random.split(key, 3)
    spots = jax.random.randint(first, (4,), 0, TIMES, dtype=jnp.int32)
    depth = jax.random.uniform(second, (4,), jnp.float32, 0.2, 0.5)
    base = 1.0 - 0.0002 * jax.random.uniform(third, (TIMES,), jnp.float32)
    steps = jnp.arange(TIMES, dtype=jnp.int32)
    hit = steps[:, None] == spots[None, :]
    factor = jnp.prod(jnp.where(hit, 1.0 - depth[None, :], 1.0), axis=1)
    return (base * factor).astype(jnp.float32)


def with_spikes(values, own_key, source, target, parts, factor):
    def block_of(axis_at):
        return (jnp.arange(values.shape[axis_at]) // (values.shape[axis_at] // parts)).reshape((-1,) + (1,) * (values.ndim - 1 - axis_at))

    near = jax.random.permutation(own_key, parts)[block_of(target)]
    far = (block_of(target) + parts // 2) % parts
    return jnp.where((block_of(source) == near) | (block_of(source) == far), factor * values, values)


def block_levels(key, extent, cuts, low, high):
    loudness, own = 1.0, jax.random.fold_in(key, 6)
    for dim, shards_of in cuts:
        steps = jnp.exp(jax.random.uniform(jax.random.fold_in(own, dim), (shards_of,), jnp.float32, low / len(cuts), high / len(cuts)))
        loudness = loudness * jnp.repeat(steps, extent[dim] // shards_of).reshape([-1 if axis == dim else 1 for axis in range(len(extent))])
    return loudness


def normal_values(stream_key, dims, deviation, limit, cuts=(), held_as=jnp.bfloat16):
    values = jax.random.normal(stream_key, dims, jnp.float32) * deviation
    if len(cuts) > 0:
        values = block_levels(stream_key, dims, cuts, -0.22, 0.18) * values
    return jnp.clip(values, min=-limit, max=limit).astype(held_as)


def heavy_noise(stream_key, extent, deviation, bound, shards, heavy, kind=jnp.bfloat16):
    entries = deviation * jax.random.normal(stream_key, extent, jnp.float32)
    if shards:
        entries = entries * block_levels(stream_key, extent, shards, -0.22, 0.18)
    return jnp.clip(with_spikes(entries, jax.random.fold_in(stream_key, 3), *heavy), -bound, bound).astype(kind)


def setup_inputs(seed: int = 0) -> dict:
    key_of = jax.random.split(jax.random.key(seed), 8)
    return {
        "loads": normal_values(key_of[0], (TIMES, LOADS), 1.0, 6.0, ((0, 4), (1, 8))),
        "phi": heavy_noise(key_of[1], (NDOF, M), LOADS ** -0.5, 0.125, ((0, 8),), (0, 1, 8, 2.0)),
        "load_index": draw_load_index(jax.random.fold_in(key_of[7], 71), 0),
        "damping": jnp.clip(jnp.exp(math.log(0.05) - 5.9506425 * jax.random.uniform(key_of[3], (M,), jnp.float32) ** block_levels(key_of[3], (M,), ((0, 8),), -0.2, 0.2)), 0.00013020834, 0.05),
        "frequency": jnp.clip(0.05 + 1.45 * jax.random.uniform(key_of[4], (M,), jnp.float32) ** block_levels(key_of[4], (M,), ((0, 8),), -0.2, 0.2), 0.05, 1.5),
        "gains": draw_gains(jax.random.fold_in(key_of[7], 71), 0),
        "shapes": normal_values(key_of[6], (M, NFP), M ** -0.5, 0.09375, ((1, 8),)),
    }


def combine(earlier, later):
    ear, eai, ebr, ebi = earlier
    lar, lai, lbr, lbi = later
    return (lar * ear - lai * eai, lar * eai + lai * ear, lar * ebr - lai * ebi + lbr, lar * ebi + lai * ebr + lbi)

def reference(loads, phi, load_index, damping, frequency, gains, shapes):
    selected = jnp.take(phi, load_index, axis=0)
    modal = jnp.dot(selected.T, loads.T, preferred_element_type=jnp.float32)
    radius = jnp.exp(-damping)
    drive = jnp.sqrt(-jnp.expm1(-2.0 * damping))
    coef_re = gains[None, :] * (radius * jnp.cos(frequency))[:, None]
    coef_im = gains[None, :] * (radius * jnp.sin(frequency))[:, None]
    push_re = drive[:, None] * modal
    push_im = jnp.zeros_like(push_re)
    result = lax.associative_scan(combine, (coef_re, coef_im, push_re, push_im), axis=1)
    history = result[2]
    rounded = history.astype(jnp.bfloat16)
    field = jnp.dot(rounded.T, shapes, preferred_element_type=jnp.float32).astype(jnp.bfloat16)
    return (field, history)
```

```python
import functools

import jax
import jax.numpy as jnp
from jax import lax
from jax.experimental import pallas as pl
from jax.experimental.pallas import tpu as pltpu
from jax.sharding import PartitionSpec as P

MESH = pl.DeviceIdType.MESH
NSUB = 2
SEGS = 8
CORE, DA, DB, XA, XB, YA, YB = 0, 4, 5, 6, 7, 8, 9
GXA, GXB, GYA, GYB, GP, FA, FB, PX, PY, PD, TM = 10, 11, 12, 13, 14, 15, 16, 17, 18, 19, 20


def cmul(ar, ai, br, bi):
    return ar * br - ai * bi, ar * bi + ai * br


def power(ar, ai, exponent):
    result = None
    while exponent:
        if exponent & 1:
            result = (ar, ai) if result is None else cmul(*result, ar, ai)
        exponent >>= 1
        if exponent:
            ar, ai = cmul(ar, ai, ar, ai)
    return result


def kernel(
    tms, pars, gains, index, loads, phi, shapes, field, hist,
    onehot, spread, phi_buf, shapes_buf, tx_core, rx_core, tx_d, tx_x, tx_y, rx_d, rx_x, rx_y,
    hold_x, hold_y, mod, tx_tm, rx_tm, carry, gath, acc, send, recv, phi_sem, shapes_sem,
):
    steps = loads.shape[0]
    half = steps // 2
    owned = pars.shape[1]
    width = owned // NSUB
    cols = width // 128
    seg = steps // SEGS
    rows = phi.shape[0]
    channels = loads.shape[1]
    points = shapes.shape[1]
    tile = min(512, points)
    top, low = pl.ds(0, half), pl.ds(half, half)

    d = lax.axis_index("dof")
    me = lax.axis_index("tm")
    core = lax.rem(d, 2)
    px = lax.rem(d // 2, 2)
    py = d // 4
    other = 1 - core
    partner = d + 1 - 2 * core
    xn = d + 2 * (1 - 2 * px)
    yn = d + 4 * (1 - 2 * py)

    def owner(q, cc):
        fx, fy = q % 2, q // 2
        x = px + fx * (1 - 2 * px)
        y = py + fy * (1 - 2 * py)
        return (y * 2 + x) * 2 + cc

    def remote(src, dst, kind, s, to):
        return pltpu.make_async_remote_copy(
            src_ref=src, dst_ref=dst, send_sem=send.at[s, kind], recv_sem=recv.at[s, kind],
            device_id={"dof": to}, device_id_type=MESH,
        )

    def core_copy(q, s):
        return remote(tx_core.at[q, s], rx_core.at[q, s], CORE + q, s, partner)

    def piece(src, dst, span, kind, s, to):
        return remote(src.at[s, span], dst.at[s, span], kind, s, to)

    def da(s):
        return piece(tx_d, rx_d, top, DA, s, xn)

    def db(s):
        return piece(tx_d, rx_d, low, DB, s, yn)

    def xa(s):
        return piece(tx_x, rx_x, top, XA, s, xn)

    def xb(s):
        return piece(tx_x, rx_x, low, XB, s, xn)

    def ya(s):
        return piece(tx_y, rx_y, top, YA, s, yn)

    def yb(s):
        return piece(tx_y, rx_y, low, YB, s, yn)

    def gathered(src, dst, span, kind, s, to):
        return remote(gath.at[src[0], src[1], s, span], gath.at[dst[0], dst[1], s, span], kind, s, to)

    whole = pl.ds(0, steps)

    def gxa(s):
        return gathered((0, 0), (1, 0), top, GXA, s, xn)

    def gxb(s):
        return gathered((0, 0), (1, 0), low, GXB, s, xn)

    def gya(s):
        return gathered((0, 0), (2, 0), top, GYA, s, yn)

    def gyb(s):
        return gathered((0, 0), (2, 0), low, GYB, s, yn)

    def gp(s):
        return gathered((0, 0), (0, 1), whole, GP, s, partner)

    def fa(s):
        return gathered((1, 0), (3, 0), top, FA, s, yn)

    def fb(s):
        return gathered((2, 0), (3, 0), low, FB, s, xn)

    def pq(q, s):
        return gathered((q, 0), (q, 1), whole, PX + q - 1, s, partner)

    def state_copy(dk, s, to):
        return pltpu.make_async_remote_copy(
            src_ref=tx_tm.at[s], dst_ref=rx_tm.at[dk - 1, s],
            send_sem=send.at[s, TM + dk - 1], recv_sem=recv.at[s, TM + dk - 1],
            device_id={"tm": to}, device_id_type=MESH,
        )

    def phi_copy(slot, q, cc, s):
        start = pl.multiple_of(owner(q, cc) * owned + s * width, width)
        return pltpu.make_async_copy(phi.at[:, pl.ds(start, width)], phi_buf.at[slot], phi_sem.at[slot])

    order = (3, 1, 2, 0)

    def start_partner_tiles(s):
        for slot in range(4):
            phi_copy(slot, 3 - slot, other, s).start()

    def start_own_tiles(s):
        for slot, q in enumerate(order):
            phi_copy(4 + slot, q, core, s).start()

    shapes_copy = pltpu.make_async_copy(shapes, shapes_buf, shapes_sem)

    barrier = pltpu.get_barrier_semaphore()
    start_partner_tiles(0)
    start_own_tiles(0)
    for to in (partner, xn, yn):
        pl.semaphore_signal(barrier, inc=1, device_id={"dof": to}, device_id_type=MESH)
    for dk in range(1, tms):
        to = lax.rem(me + dk, tms)
        pl.semaphore_signal(barrier, inc=1, device_id={"tm": to}, device_id_type=MESH)

    place = lax.broadcasted_iota(jnp.int32, (rows, channels), 0)
    hit = jnp.where(place == index[...] - d * rows, 1.0, 0.0).astype(jnp.float32)
    onehot[...] = hit.T.astype(jnp.bfloat16)
    spread[...] = jnp.broadcast_to(gains[...], (128, steps)).T
    pl.semaphore_wait(barrier, 3 + tms - 1)

    def partial_modal(slot):
        chosen = jnp.dot(onehot[...], phi_buf[slot], preferred_element_type=jnp.float32)
        return jnp.dot(loads[...], chosen.astype(jnp.bfloat16), preferred_element_type=jnp.float32)

    def for_partner(s):
        def one(slot, _):
            q = 3 - slot
            phi_copy(slot, q, other, s).wait()
            tx_core[q, s] = partial_modal(slot).astype(jnp.bfloat16)
            core_copy(q, s).start()
            return 0

        lax.fori_loop(0, 4, one, 0)

    def own_sum(slot, q, s):
        phi_copy(4 + slot, q, core, s).wait()
        value = partial_modal(4 + slot)
        core_copy(q, s).wait_recv()
        return value + rx_core[q, s].astype(jnp.float32)

    def for_chips(s):
        tx_d[s] = own_sum(0, 3, s).astype(jnp.bfloat16)
        da(s).start()
        db(s).start()
        value = own_sum(1, 1, s)
        tx_x[s, :half] = value[:half].astype(jnp.bfloat16)
        xa(s).start()
        hold_x[s] = value[half:]
        value = own_sum(2, 2, s)
        tx_y[s, half:] = value[half:].astype(jnp.bfloat16)
        yb(s).start()
        hold_y[s] = value[:half]
        value = own_sum(3, 0, s)
        for j in range(cols):
            mod[s, j] = value[:, j * 128:(j + 1) * 128]

    def pass_on(s):
        db(s).wait_recv()
        tx_x[s, half:] = (hold_x[s] + rx_d[s, half:].astype(jnp.float32)).astype(jnp.bfloat16)
        xb(s).start()
        da(s).wait_recv()
        tx_y[s, :half] = (hold_y[s] + rx_d[s, :half].astype(jnp.float32)).astype(jnp.bfloat16)
        ya(s).start()

    def par(s, j):
        lanes = slice(s * width + j * 128, s * width + (j + 1) * 128)
        return pars[0:1, lanes], pars[1:2, lanes], pars[2:3, lanes]

    def scan(s, start, store):
        coefs = [tuple(jnp.broadcast_to(v, (SEGS, 128)) for v in par(s, j)[:2]) for j in range(cols)]

        def step(i, state):
            total, waves = state
            at = pl.ds(i, SEGS, stride=seg)
            gain = spread[at, :]
            out = []
            for j in range(cols):
                re, im = cmul(*coefs[j], *waves[j])
                re = gain * re + mod[s, j, at, :]
                im = gain * im
                if store:
                    mod[s, j, at, :] = re
                out.append((re, im))
            return total * gain, tuple(out)

        one = jnp.ones((SEGS, 128), jnp.float32)
        return lax.fori_loop(0, seg, step, (one, tuple(start)), unroll=8)

    def local_states(s):
        for copy in (xa(s), xb(s), ya(s), yb(s)):
            copy.wait_recv()
        for j in range(cols):
            lanes = slice(j * 128, (j + 1) * 128)
            value = mod[s, j] + rx_x[s, :, lanes].astype(jnp.float32) + rx_y[s, :, lanes].astype(jnp.float32)
            mod[s, j] = value * par(s, j)[2]
        zero = jnp.zeros((SEGS, 128), jnp.float32)
        total, ends = scan(s, [(zero, zero)] * cols, False)
        kept = []
        for j in range(cols):
            lanes = slice(j * 128, (j + 1) * 128)
            a, b, _ = par(s, j)
            ar, ai = power(a, b, seg)
            state = (jnp.zeros((1, 128), jnp.float32),) * 2
            prod = (jnp.ones((1, 128), jnp.float32), jnp.zeros((1, 128), jnp.float32))
            entering, products = [], []
            gain = jnp.ones((1, 128), jnp.float32)
            for k in range(SEGS):
                entering.append(state)
                products.append(prod)
                g = total[k:k + 1]
                c = (ar * g, ai * g)
                moved = cmul(*c, *state)
                state = (moved[0] + ends[j][0][k:k + 1], moved[1] + ends[j][1][k:k + 1])
                prod = cmul(*c, *prod)
                gain = gain * g
            tx_tm[s, 0:1, lanes] = state[0]
            tx_tm[s, 1:2, lanes] = state[1]
            tx_tm[s, 2:3, lanes] = gain
            kept.append(tuple(
                jnp.concatenate([v[n] for v in some], axis=0) for some in (entering, products) for n in (0, 1)
            ))
        for dk in range(1, tms):
            @pl.when(me + dk < tms)
            def _():
                state_copy(dk, s, me + dk).start()
        return kept

    def finish(s, kept):
        carry[s] = jnp.zeros(carry.shape[1:], jnp.float32)
        for dk in range(tms - 1, 0, -1):
            @pl.when(me >= dk)
            def _():
                state_copy(dk, s, me).wait_recv()
                for j in range(cols):
                    lanes = slice(j * 128, (j + 1) * 128)
                    a, b, _ = par(s, j)
                    ar, ai = power(a, b, steps)
                    gain = rx_tm[dk - 1, s, 2:3, lanes]
                    re, im = cmul(ar * gain, ai * gain, carry[s, 0:1, lanes], carry[s, 1:2, lanes])
                    carry[s, 0:1, lanes] = re + rx_tm[dk - 1, s, 0:1, lanes]
                    carry[s, 1:2, lanes] = im + rx_tm[dk - 1, s, 1:2, lanes]
        start = []
        for j in range(cols):
            lanes = slice(j * 128, (j + 1) * 128)
            er, ei, kr, ki = kept[j]
            re, im = cmul(kr, ki, carry[s, 0:1, lanes], carry[s, 1:2, lanes])
            start.append((er + re, ei + im))
        scan(s, start, True)
        for j in range(cols):
            gath[0, 0, s, :, j * 128:(j + 1) * 128] = mod[s, j].astype(jnp.bfloat16)
        for copy in (gxa(s), gyb(s), gp(s), gxb(s), gya(s)):
            copy.start()
        for j in range(cols):
            hist[s * width + j * 128:s * width + (j + 1) * 128, :] = mod[s, j].T

    def forward(s):
        gxa(s).wait_recv()
        fa(s).start()
        gyb(s).wait_recv()
        fb(s).start()

    def share(s):
        gxb(s).wait_recv()
        pq(1, s).start()
        gya(s).wait_recv()
        pq(2, s).start()

    def share_last(s):
        fa(s).wait_recv()
        fb(s).wait_recv()
        pq(3, s).start()

    def expand(q, s, mode):
        mine = pl.multiple_of(owner(q, core) * owned + s * width, width)
        theirs = pl.multiple_of(owner(q, other) * owned + s * width, width)

        def one(n, _):
            at = pl.ds(pl.multiple_of(n * tile, tile), tile)
            value = jnp.dot(gath[q, 0, s], shapes_buf[pl.ds(mine, width), at], preferred_element_type=jnp.float32)
            value += jnp.dot(gath[q, 1, s], shapes_buf[pl.ds(theirs, width), at], preferred_element_type=jnp.float32)
            if mode != "first":
                value += acc[:, at]
            if mode == "last":
                field[:, at] = value.astype(jnp.bfloat16)
            else:
                acc[:, at] = value
            return 0

        lax.fori_loop(0, points // tile, one, 0)

    for_partner(0)
    start_partner_tiles(1)
    for_chips(0)
    start_own_tiles(1)
    shapes_copy.start()
    for_partner(1)
    pass_on(0)
    for_chips(1)
    kept_0 = local_states(0)
    pass_on(1)
    finish(0, kept_0)
    kept_1 = local_states(1)
    forward(0)
    finish(1, kept_1)
    share(0)
    shapes_copy.wait()
    gp(0).wait_recv()
    expand(0, 0, "first")
    forward(1)
    share_last(0)
    gp(1).wait_recv()
    expand(0, 1, "add")
    pq(1, 0).wait_recv()
    expand(1, 0, "add")
    share(1)
    pq(2, 0).wait_recv()
    expand(2, 0, "add")
    pq(3, 0).wait_recv()
    expand(3, 0, "add")
    pq(1, 1).wait_recv()
    expand(1, 1, "add")
    share_last(1)
    pq(2, 1).wait_recv()
    expand(2, 1, "add")
    pq(3, 1).wait_recv()
    expand(3, 1, "last")

    for s in range(NSUB):
        for q in range(4):
            core_copy(q, s).wait_send()
        for copy in (
            da(s), db(s), xa(s), xb(s), ya(s), yb(s), gxa(s), gxb(s), gya(s), gyb(s), gp(s), fa(s), fb(s),
            pq(1, s), pq(2, s), pq(3, s),
        ):
            copy.wait_send()
        for dk in range(1, tms):
            @pl.when(me + dk < tms)
            def _():
                state_copy(dk, s, me).wait_send()


def fused(tms, loads, phi, load_index, damping, frequency, gains, shapes):
    owned, steps, channels = damping.shape[0], loads.shape[0], loads.shape[1]
    rows, points, modes = phi.shape[0], shapes.shape[1], shapes.shape[0]
    width = owned // NSUB
    half = steps // 2
    radius = jnp.exp(-damping)
    drive = jnp.sqrt(-jnp.expm1(-2.0 * damping))
    pars = jnp.stack([radius * jnp.cos(frequency), radius * jnp.sin(frequency), drive])
    b16, f32 = jnp.bfloat16, jnp.float32
    kinds = TM + tms - 1
    small = pl.BlockSpec(memory_space=pltpu.VMEM)
    large = pl.BlockSpec(memory_space=pl.ANY)
    return pl.pallas_call(
        functools.partial(kernel, tms),
        out_shape=(
            jax.ShapeDtypeStruct((steps, points), b16),
            jax.ShapeDtypeStruct((owned, steps), f32),
        ),
        in_specs=[small, small, small, small, large, large],
        out_specs=(small, small),
        scratch_shapes=[
            pltpu.VMEM((channels, rows), b16),
            pltpu.VMEM((steps, 128), f32),
            pltpu.VMEM((8, rows, width), b16),
            pltpu.VMEM((modes, points), b16),
            pltpu.VMEM((4, NSUB, steps, width), b16),
            pltpu.VMEM((4, NSUB, steps, width), b16),
        ] + [pltpu.VMEM((NSUB, steps, width), b16)] * 6 + [
            pltpu.VMEM((NSUB, half, width), f32),
            pltpu.VMEM((NSUB, half, width), f32),
            pltpu.VMEM((NSUB, width // 128, steps, 128), f32),
            pltpu.VMEM((NSUB, 8, width), f32),
            pltpu.VMEM((tms - 1, NSUB, 8, width), f32),
            pltpu.VMEM((NSUB, 8, width), f32),
            pltpu.VMEM((4, 2, NSUB, steps, width), b16),
            pltpu.VMEM((steps, points), f32),
            pltpu.SemaphoreType.DMA((NSUB, kinds)),
            pltpu.SemaphoreType.DMA((NSUB, kinds)),
            pltpu.SemaphoreType.DMA((8,)),
            pltpu.SemaphoreType.DMA,
        ],
        compiler_params=pltpu.CompilerParams(
            collective_id=0, has_side_effects=True, vmem_limit_bytes=56 * 1024 * 1024
        ),
        cost_estimate=pl.CostEstimate(
            flops=2 * steps * modes * (points + channels) + 2 * channels * rows * modes,
            bytes_accessed=2 * (modes * points + rows * modes + steps * points),
            transcendentals=0,
        ),
    )(pars, gains.reshape(1, steps), load_index.reshape(1, channels), loads, phi, shapes)


def carried_in(value, axis, join, neutral):
    count, mine = (lax.axis_size(axis), lax.axis_index(axis))
    pieces = jax.tree.map(lambda part: lax.all_gather(part, axis), value)
    subtotal = jax.tree.map(
        lambda part, zero: jnp.full_like(part, 0) + jnp.asarray(zero, part.dtype), value, neutral
    )

    def step(position, subtotal):
        longer = join(subtotal, jax.tree.map(lambda part: part[position], pieces))
        return jax.tree.map(lambda new, old: jnp.where(position < mine, new, old), longer, subtotal)

    return lax.fori_loop(0, count - 1, step, subtotal)


def combine(earlier, later):
    ear, eai, ebr, ebi = earlier
    lar, lai, lbr, lbi = later
    return (
        lar * ear - lai * eai,
        lar * eai + lai * ear,
        lar * ebr - lai * ebi + lbr,
        lar * ebi + lai * ebr + lbi,
    )


def body(loads, phi, load_index, damping, frequency, gains, shapes):
    owned = damping.shape[0]
    steps = loads.shape[0]
    rows_here = phi.shape[0]
    local_index = load_index - lax.axis_index("dof") * rows_here
    selected = jnp.take(phi, local_index, axis=0)
    columns = lax.all_to_all(selected, "dof", split_axis=1, concat_axis=0, tiled=True)
    block = columns
    modal = lax.dot_general(
        block,
        lax.all_gather(loads, "dof", axis=1, tiled=True),
        (((0,), (1,)), ((), ())),
        preferred_element_type=jnp.float32,
    )
    drive = jnp.sqrt(-jnp.expm1(-2.0 * damping))
    width = min(128, steps)
    blocks = steps // width
    log_gain = jnp.cumsum(jnp.log(gains).reshape(blocks, width), axis=1)
    rise = jnp.exp(log_gain)
    fall = jnp.exp(-log_gain)
    offsets = jnp.arange(width, dtype=jnp.float32)
    lag = offsets[:, None] - offsets[None, :]
    lower = lag >= 0.0
    lag_pos = jnp.where(lower, lag, 0.0)
    decay = jnp.exp(-damping[:, None, None] * lag_pos[None, :, :])
    turn = frequency[:, None, None] * lag_pos[None, :, :]
    kernel_re = jnp.where(lower[None, :, :], decay * jnp.cos(turn), 0.0)
    kernel_im = jnp.where(lower[None, :, :], decay * jnp.sin(turn), 0.0)
    pushed = (drive[:, None] * modal).reshape(owned, blocks, width) * fall[None, :, :]
    local_re = (
        jnp.einsum("mts,mns->mnt", kernel_re, pushed, precision=lax.Precision.HIGHEST)
        * rise[None, :, :]
    )
    local_im = (
        jnp.einsum("mts,mns->mnt", kernel_im, pushed, precision=lax.Precision.HIGHEST)
        * rise[None, :, :]
    )
    ahead = offsets + 1.0
    power_mag = jnp.exp(-damping[:, None] * ahead[None, :])
    power_re = power_mag * jnp.cos(frequency[:, None] * ahead[None, :])
    power_im = power_mag * jnp.sin(frequency[:, None] * ahead[None, :])
    carry_re_all = power_re[:, None, :] * rise[None, :, :]
    carry_im_all = power_im[:, None, :] * rise[None, :, :]
    unit = jnp.ones((owned,), jnp.float32)
    nothing = jnp.zeros((owned,), jnp.float32)
    running = (unit, nothing, nothing, nothing)
    entering = []
    for index in range(blocks):
        entering.append(running)
        piece = (
            carry_re_all[:, index, width - 1],
            carry_im_all[:, index, width - 1],
            local_re[:, index, width - 1],
            local_im[:, index, width - 1],
        )
        running = combine(running, piece)
    incoming = carried_in(running, "tm", combine, (unit, nothing, nothing, nothing))
    state_re = []
    state_im = []
    for index in range(blocks):
        joined = combine(incoming, entering[index])
        state_re.append(joined[2])
        state_im.append(joined[3])
    enter_re = jnp.stack(state_re, axis=1)
    enter_im = jnp.stack(state_im, axis=1)
    history = (
        carry_re_all * enter_re[:, :, None] - carry_im_all * enter_im[:, :, None] + local_re
    ).reshape(owned, steps)
    rounded = history.astype(jnp.bfloat16)
    block = shapes
    field = lax.dot_general(
        lax.all_gather(rounded, "dof", axis=0, tiled=True),
        block,
        (((0,), (0,)), ((), ())),
        preferred_element_type=jnp.float32,
    )
    return (field.astype(jnp.bfloat16), history)


def solution(mesh):
    placed = (P("tm", "dof"), P("dof", None), P("dof"), P("dof"), P("dof"), P("tm"), P(None, "dof"))
    part = functools.partial(fused, mesh.shape["tm"]) if mesh.shape["dof"] == 8 else body
    return jax.shard_map(
        part,
        mesh=mesh,
        in_specs=placed,
        out_specs=(P("tm", "dof"), P("dof", "tm")),
        check_vma=False,
    )
```

```python
import functools

import jax
import jax.numpy as jnp
from jax import lax
from jax.experimental import pallas as pl
from jax.experimental.pallas import tpu as pltpu
from jax.sharding import PartitionSpec as P

MESH = pl.DeviceIdType.MESH
NSUB = 2
SEGS = 8
CORE, DA, DB, XA, XB, YA, YB = 0, 4, 5, 6, 7, 8, 9
GXA, GXB, GYA, GYB, GP, FA, FB, PX, PY, PD, TM = 10, 11, 12, 13, 14, 15, 16, 17, 18, 19, 20


def cmul(ar, ai, br, bi):
    return ar * br - ai * bi, ar * bi + ai * br


def power(ar, ai, exponent):
    result = None
    while exponent:
        if exponent & 1:
            result = (ar, ai) if result is None else cmul(*result, ar, ai)
        exponent >>= 1
        if exponent:
            ar, ai = cmul(ar, ai, ar, ai)
    return result


def kernel(
    tms, damping, frequency, gains, index, loads_in, phi, shapes, field, hist,
    pars, onehot, spread, loads, phi_buf, shapes_buf, tx_core, rx_core, own, tx_d, tx_x, tx_y, rx_d, rx_x, rx_y,
    mod, tx_tm, rx_tm, carry, gath, acc, turned, rounded,
    send, recv, loads_sem, phi_sem, shapes_sem, turned_sem, field_sem,
):
    steps = loads.shape[0]
    half = steps // 2
    owned = pars.shape[1]
    width = owned // NSUB
    cols = width // 128
    seg = steps // SEGS
    rows = phi.shape[0]
    channels = loads.shape[1]
    points = shapes.shape[1]
    tile = min(512, points)
    top, low = pl.ds(0, half), pl.ds(half, half)

    d = lax.axis_index("dof")
    me = lax.axis_index("tm")
    core = lax.rem(d, 2)
    px = lax.rem(d // 2, 2)
    py = d // 4
    other = 1 - core
    partner = d + 1 - 2 * core
    xn = d + 2 * (1 - 2 * px)
    yn = d + 4 * (1 - 2 * py)

    def owner(q, cc):
        fx, fy = q % 2, q // 2
        x = px + fx * (1 - 2 * px)
        y = py + fy * (1 - 2 * py)
        return (y * 2 + x) * 2 + cc

    def remote(src, dst, kind, s, to):
        return pltpu.make_async_remote_copy(
            src_ref=src, dst_ref=dst, send_sem=send.at[s, kind], recv_sem=recv.at[s, kind],
            device_id={"dof": to}, device_id_type=MESH,
        )

    def core_copy(q, s):
        return remote(tx_core.at[q, s], rx_core.at[q, s], CORE + q, s, partner)

    def piece(src, dst, span, kind, s, to):
        return remote(src.at[s, span], dst.at[s, span], kind, s, to)

    def da(s):
        return piece(tx_d, rx_d, top, DA, s, xn)

    def db(s):
        return piece(tx_d, rx_d, low, DB, s, yn)

    def xa(s):
        return piece(tx_x, rx_x, top, XA, s, xn)

    def xb(s):
        return piece(tx_x, rx_x, low, XB, s, xn)

    def ya(s):
        return piece(tx_y, rx_y, top, YA, s, yn)

    def yb(s):
        return piece(tx_y, rx_y, low, YB, s, yn)

    def lanes_of(q, r, s):
        return pl.ds(((s * 4 + q) * 2 + r) * width, width)

    def gathered(src, dst, span, kind, s, to):
        return remote(gath.at[span, lanes_of(*src, s)], gath.at[span, lanes_of(*dst, s)], kind, s, to)

    whole = pl.ds(0, steps)

    def gxa(s):
        return gathered((0, 0), (1, 0), top, GXA, s, xn)

    def gxb(s):
        return gathered((0, 0), (1, 0), low, GXB, s, xn)

    def gya(s):
        return gathered((0, 0), (2, 0), top, GYA, s, yn)

    def gyb(s):
        return gathered((0, 0), (2, 0), low, GYB, s, yn)

    def gp(s):
        return gathered((0, 0), (0, 1), whole, GP, s, partner)

    def fa(s):
        return gathered((1, 0), (3, 0), top, FA, s, yn)

    def fb(s):
        return gathered((2, 0), (3, 0), low, FB, s, xn)

    def pq(q, s):
        return gathered((q, 0), (q, 1), whole, PX + q - 1, s, partner)

    def state_copy(dk, s, to):
        return pltpu.make_async_remote_copy(
            src_ref=tx_tm.at[s], dst_ref=rx_tm.at[dk - 1, s],
            send_sem=send.at[s, TM + dk - 1], recv_sem=recv.at[s, TM + dk - 1],
            device_id={"tm": to}, device_id_type=MESH,
        )

    def phi_copy(q, r, s):
        start = pl.multiple_of(owner(q, other if r else core) * owned + s * width, width)
        return pltpu.make_async_copy(
            phi.at[:, pl.ds(start, width)], phi_buf.at[s, q, r], phi_sem.at[s, q, r]
        )

    def shapes_copy(q, r, s):
        start = pl.multiple_of(owner(q, other if r else core) * owned + s * width, width)
        return pltpu.make_async_copy(
            shapes.at[pl.ds(start, width), :], shapes_buf.at[lanes_of(q, r, s), :], shapes_sem.at[s, q, r]
        )

    loads_copy = pltpu.make_async_copy(loads_in, loads, loads_sem)
    order = (3, 1, 2, 0)

    barrier = pltpu.get_barrier_semaphore()
    for to in (partner, xn, yn):
        pl.semaphore_signal(barrier, inc=1, device_id={"dof": to}, device_id_type=MESH)
    for dk in range(1, tms):
        to = lax.rem(me + dk, tms)
        pl.semaphore_signal(barrier, inc=1, device_id={"tm": to}, device_id_type=MESH)
    loads_copy.start()
    for s in range(NSUB):
        for q in order:
            phi_copy(q, 1, s).start()
            phi_copy(q, 0, s).start()

    names = jnp.broadcast_to(index[...] - d * rows, (128, channels)).T
    for j in range(rows // 128):
        place = lax.broadcasted_iota(jnp.int32, (channels, 128), 1) + j * 128
        onehot[:, j * 128:(j + 1) * 128] = jnp.where(place == names, 1.0, 0.0).astype(jnp.bfloat16)
    loads_copy.wait()

    def partial_modal(q, r, s):
        phi_copy(q, r, s).wait()
        chosen = jnp.dot(onehot[...], phi_buf[s, q, r], preferred_element_type=jnp.float32)
        return jnp.dot(loads[...], chosen.astype(jnp.bfloat16), preferred_element_type=jnp.float32)

    def for_partner(q, s):
        tx_core[q, s] = partial_modal(q, 1, s).astype(jnp.bfloat16)
        if q == order[0] and s == 0:
            pl.semaphore_wait(barrier, 3 + tms - 1)
        core_copy(q, s).start()

    def chip_sum(q, s, span):
        return own[s, q, span] + rx_core[q, s, span].astype(jnp.float32)

    def to_chip(q, s):
        core_copy(q, s).wait_recv()
        if q == 3:
            tx_d[s] = chip_sum(q, s, pl.ds(0, steps)).astype(jnp.bfloat16)
            da(s).start()
            db(s).start()
        if q == 1:
            tx_x[s, top] = chip_sum(q, s, top).astype(jnp.bfloat16)
            xa(s).start()
        if q == 2:
            tx_y[s, low] = chip_sum(q, s, low).astype(jnp.bfloat16)
            yb(s).start()

    def partials(s, between=None):
        for n, q in enumerate(order):
            for_partner(q, s)
            if n:
                to_chip(order[n - 1], s)
            if between is not None and n == 2:
                between()
            own[s, q] = partial_modal(q, 0, s)

    def parameters():
        x = 2.0 * damping[...]
        series = jnp.ones_like(x)
        for n in range(12, 1, -1):
            series = 1.0 - x * series / n
        drive = jnp.sqrt(jnp.where(x < 0.5, x * series, 1.0 - jnp.exp(-x)))
        radius = jnp.exp(-damping[...])
        pars[0:1, :] = radius * jnp.cos(frequency[...])
        pars[1:2, :] = radius * jnp.sin(frequency[...])
        pars[2:3, :] = drive
        spread[...] = jnp.broadcast_to(gains[...].reshape(1, steps), (128, steps)).T

    def pass_on(s):
        db(s).wait_recv()
        tx_x[s, low] = (chip_sum(1, s, low) + rx_d[s, low].astype(jnp.float32)).astype(jnp.bfloat16)
        xb(s).start()
        da(s).wait_recv()
        tx_y[s, top] = (chip_sum(2, s, top) + rx_d[s, top].astype(jnp.float32)).astype(jnp.bfloat16)
        ya(s).start()

    def par(s, j):
        lanes = slice(s * width + j * 128, s * width + (j + 1) * 128)
        return pars[0:1, lanes], pars[1:2, lanes], pars[2:3, lanes]

    def scan(s, start, store):
        coefs = [tuple(jnp.broadcast_to(v, (SEGS, 128)) for v in par(s, j)[:2]) for j in range(cols)]

        def step(i, state):
            total, waves = state
            at = pl.ds(i, SEGS, stride=seg)
            gain = spread[at, :]
            out = []
            for j in range(cols):
                re, im = cmul(*coefs[j], *waves[j])
                re = gain * re + mod[s, j, at, :]
                im = gain * im
                if store:
                    mod[s, j, at, :] = re
                out.append((re, im))
            return total * gain, tuple(out)

        one = jnp.ones((SEGS, 128), jnp.float32)
        return lax.fori_loop(0, seg, step, (one, tuple(start)), unroll=8)

    def local_states(s):
        for copy in (core_copy(0, s), xa(s), xb(s), ya(s), yb(s)):
            copy.wait_recv()
        for j in range(cols):
            lanes = slice(j * 128, (j + 1) * 128)
            value = own[s, 0, :, lanes]
            for part in (rx_core.at[0], rx_x, rx_y):
                value += part[s, :, lanes].astype(jnp.float32)
            mod[s, j] = value * par(s, j)[2]
        zero = jnp.zeros((SEGS, 128), jnp.float32)
        total, ends = scan(s, [(zero, zero)] * cols, False)
        kept = []
        for j in range(cols):
            lanes = slice(j * 128, (j + 1) * 128)
            a, b, _ = par(s, j)
            ar, ai = power(a, b, seg)
            state = (jnp.zeros((1, 128), jnp.float32),) * 2
            prod = (jnp.ones((1, 128), jnp.float32), jnp.zeros((1, 128), jnp.float32))
            entering, products = [], []
            gain = jnp.ones((1, 128), jnp.float32)
            for k in range(SEGS):
                entering.append(state)
                products.append(prod)
                g = total[k:k + 1]
                c = (ar * g, ai * g)
                moved = cmul(*c, *state)
                state = (moved[0] + ends[j][0][k:k + 1], moved[1] + ends[j][1][k:k + 1])
                prod = cmul(*c, *prod)
                gain = gain * g
            tx_tm[s, 0:1, lanes] = state[0]
            tx_tm[s, 1:2, lanes] = state[1]
            tx_tm[s, 2:3, lanes] = gain
            kept.append(tuple(
                jnp.concatenate([v[n] for v in some], axis=0) for some in (entering, products) for n in (0, 1)
            ))
        for dk in range(1, tms):
            @pl.when(me + dk < tms)
            def _():
                state_copy(dk, s, me + dk).start()
        return kept

    def finish(s, kept):
        carry[s] = jnp.zeros(carry.shape[1:], jnp.float32)
        for dk in range(tms - 1, 0, -1):
            @pl.when(me >= dk)
            def _():
                state_copy(dk, s, me).wait_recv()
                for j in range(cols):
                    lanes = slice(j * 128, (j + 1) * 128)
                    a, b, _ = par(s, j)
                    ar, ai = power(a, b, steps)
                    gain = rx_tm[dk - 1, s, 2:3, lanes]
                    re, im = cmul(ar * gain, ai * gain, carry[s, 0:1, lanes], carry[s, 1:2, lanes])
                    carry[s, 0:1, lanes] = re + rx_tm[dk - 1, s, 0:1, lanes]
                    carry[s, 1:2, lanes] = im + rx_tm[dk - 1, s, 1:2, lanes]
        start = []
        for j in range(cols):
            lanes = slice(j * 128, (j + 1) * 128)
            er, ei, kr, ki = kept[j]
            re, im = cmul(kr, ki, carry[s, 0:1, lanes], carry[s, 1:2, lanes])
            start.append((er + re, ei + im))
        scan(s, start, True)
        for j in range(cols):
            gath[:, pl.ds(s * 8 * width + j * 128, 128)] = mod[s, j].astype(jnp.bfloat16)
        for copy in (gxa(s), gyb(s), gp(s), gxb(s), gya(s)):
            copy.start()
        for j in range(cols):
            turned[s * width + j * 128:s * width + (j + 1) * 128, :] = mod[s, j].T
        turned_copy(s).start()

    def turned_copy(s):
        at = pl.ds(s * width, width)
        return pltpu.make_async_copy(turned.at[at], hist.at[at], turned_sem.at[s])

    def forward(s):
        gxa(s).wait_recv()
        fa(s).start()
        gyb(s).wait_recv()
        fb(s).start()

    def share(s):
        gxb(s).wait_recv()
        pq(1, s).start()
        gya(s).wait_recv()
        pq(2, s).start()

    def share_last(s):
        fa(s).wait_recv()
        fb(s).wait_recv()
        pq(3, s).start()

    def field_copy(n):
        at = pl.ds(pl.multiple_of(n * tile, tile), tile)
        return pltpu.make_async_copy(rounded.at[:, at], field.at[:, at], field_sem.at[n])

    def expand(first, count, mode):
        for block in range(first, first + count):
            s, q = block // 4, block % 4
            shapes_copy(q, 0, s).wait()
            shapes_copy(q, 1, s).wait()
        deep = pl.ds(first * 2 * width, count * 2 * width)

        def one(n, _):
            at = pl.ds(pl.multiple_of(n * tile, tile), tile)
            value = jnp.dot(gath[:, deep], shapes_buf[deep, at], preferred_element_type=jnp.float32)
            if mode != "first":
                value += acc[:, at]
            if mode == "last":
                rounded[:, at] = value.astype(jnp.bfloat16)
                field_copy(n).start()
            else:
                acc[:, at] = value
            return 0

        lax.fori_loop(0, points // tile, one, 0)

    partials(0)
    for s in range(NSUB):
        for q in range(4):
            shapes_copy(q, 0, s).start()
            shapes_copy(q, 1, s).start()
    parameters()
    partials(1, lambda: pass_on(0))
    kept_0 = local_states(0)
    pass_on(1)
    finish(0, kept_0)
    kept_1 = local_states(1)
    gp(0).wait_recv()
    expand(0, 1, "first")
    forward(0)
    finish(1, kept_1)
    share(0)
    share_last(0)
    pq(1, 0).wait_recv()
    pq(2, 0).wait_recv()
    expand(1, 2, "add")
    forward(1)
    pq(3, 0).wait_recv()
    gp(1).wait_recv()
    expand(3, 2, "add")
    share(1)
    share_last(1)
    pq(1, 1).wait_recv()
    pq(2, 1).wait_recv()
    expand(5, 2, "add")
    pq(3, 1).wait_recv()
    expand(7, 1, "last")

    for n in range(points // tile):
        field_copy(n).wait()
    for s in range(NSUB):
        turned_copy(s).wait()
    for s in range(NSUB):
        for q in range(4):
            core_copy(q, s).wait_send()
        for copy in (
            da(s), db(s), xa(s), xb(s), ya(s), yb(s), gxa(s), gxb(s), gya(s), gyb(s), gp(s), fa(s), fb(s),
            pq(1, s), pq(2, s), pq(3, s),
        ):
            copy.wait_send()
        for dk in range(1, tms):
            @pl.when(me + dk < tms)
            def _():
                state_copy(dk, s, me).wait_send()


def hand_over(*arrays):
    pieces = 4

    def copies(*refs):
        count = len(arrays)
        started = []
        for n in range(count):
            rows = arrays[n].shape[0] // pieces
            for piece in range(pieces):
                at = pl.ds(piece * rows, rows)
                started.append(
                    pltpu.make_async_copy(refs[n].at[at], refs[count + n].at[at], refs[2 * count].at[n, piece])
                )
        for copy in started:
            copy.start()
        for copy in started:
            copy.wait()

    large = pl.BlockSpec(memory_space=pltpu.HBM)
    return pl.pallas_call(
        copies,
        out_shape=tuple(jax.ShapeDtypeStruct(a.shape, a.dtype) for a in arrays),
        in_specs=[large] * len(arrays),
        out_specs=(large,) * len(arrays),
        scratch_shapes=[pltpu.SemaphoreType.DMA((len(arrays), pieces))],
        cost_estimate=pl.CostEstimate(
            flops=0, bytes_accessed=sum(2 * a.size * a.dtype.itemsize for a in arrays), transcendentals=0
        ),
    )(*arrays)


def fused(tms, loads, phi, load_index, damping, frequency, gains, shapes):
    owned, steps, channels = damping.shape[0], loads.shape[0], loads.shape[1]
    rows, points, modes = phi.shape[0], shapes.shape[1], shapes.shape[0]
    width = owned // NSUB
    b16, f32 = jnp.bfloat16, jnp.float32
    kinds = TM + tms - 1
    small = pl.BlockSpec(memory_space=pltpu.VMEM)
    large = pl.BlockSpec(memory_space=pl.ANY)
    results = pl.pallas_call(
        functools.partial(kernel, tms),
        out_shape=(
            jax.ShapeDtypeStruct((steps, points), b16),
            jax.ShapeDtypeStruct((owned, steps), f32),
        ),
        in_specs=[small, small, small, small, large, large, large],
        out_specs=(large, large),
        scratch_shapes=[
            pltpu.VMEM((8, owned), f32),
            pltpu.VMEM((channels, rows), b16),
            pltpu.VMEM((steps, 128), f32),
            pltpu.VMEM((steps, channels), b16),
            pltpu.VMEM((NSUB, 4, 2, rows, width), b16),
            pltpu.VMEM((modes, points), b16),
            pltpu.VMEM((4, NSUB, steps, width), b16),
            pltpu.VMEM((4, NSUB, steps, width), b16),
            pltpu.VMEM((NSUB, 4, steps, width), f32),
        ] + [pltpu.VMEM((NSUB, steps, width), b16)] * 6 + [
            pltpu.VMEM((NSUB, width // 128, steps, 128), f32),
            pltpu.VMEM((NSUB, 8, width), f32),
            pltpu.VMEM((tms - 1, NSUB, 8, width), f32),
            pltpu.VMEM((NSUB, 8, width), f32),
            pltpu.VMEM((steps, modes), b16),
            pltpu.VMEM((steps, points), f32),
            pltpu.VMEM((owned, steps), f32),
            pltpu.VMEM((steps, points), b16),
            pltpu.SemaphoreType.DMA((NSUB, kinds)),
            pltpu.SemaphoreType.DMA((NSUB, kinds)),
            pltpu.SemaphoreType.DMA,
            pltpu.SemaphoreType.DMA((NSUB, 4, 2)),
            pltpu.SemaphoreType.DMA((NSUB, 4, 2)),
            pltpu.SemaphoreType.DMA((NSUB,)),
            pltpu.SemaphoreType.DMA((points // min(512, points),)),
        ],
        compiler_params=pltpu.CompilerParams(
            collective_id=0, has_side_effects=True, vmem_limit_bytes=56 * 1024 * 1024
        ),
        cost_estimate=pl.CostEstimate(
            flops=2 * steps * modes * (points + channels) + 2 * channels * rows * modes,
            bytes_accessed=2 * (modes * points + rows * modes + steps * points),
            transcendentals=0,
        ),
    )(damping.reshape(1, owned), frequency.reshape(1, owned), gains, load_index.reshape(1, channels), loads, phi, shapes)
    return hand_over(*results)


def carried_in(value, axis, join, neutral):
    count, mine = (lax.axis_size(axis), lax.axis_index(axis))
    pieces = jax.tree.map(lambda part: lax.all_gather(part, axis), value)
    subtotal = jax.tree.map(
        lambda part, zero: jnp.full_like(part, 0) + jnp.asarray(zero, part.dtype), value, neutral
    )

    def step(position, subtotal):
        longer = join(subtotal, jax.tree.map(lambda part: part[position], pieces))
        return jax.tree.map(lambda new, old: jnp.where(position < mine, new, old), longer, subtotal)

    return lax.fori_loop(0, count - 1, step, subtotal)


def combine(earlier, later):
    ear, eai, ebr, ebi = earlier
    lar, lai, lbr, lbi = later
    return (
        lar * ear - lai * eai,
        lar * eai + lai * ear,
        lar * ebr - lai * ebi + lbr,
        lar * ebi + lai * ebr + lbi,
    )


def body(loads, phi, load_index, damping, frequency, gains, shapes):
    owned = damping.shape[0]
    steps = loads.shape[0]
    rows_here = phi.shape[0]
    local_index = load_index - lax.axis_index("dof") * rows_here
    selected = jnp.take(phi, local_index, axis=0)
    columns = lax.all_to_all(selected, "dof", split_axis=1, concat_axis=0, tiled=True)
    block = columns
    modal = lax.dot_general(
        block,
        lax.all_gather(loads, "dof", axis=1, tiled=True),
        (((0,), (1,)), ((), ())),
        preferred_element_type=jnp.float32,
    )
    drive = jnp.sqrt(-jnp.expm1(-2.0 * damping))
    width = min(128, steps)
    blocks = steps // width
    log_gain = jnp.cumsum(jnp.log(gains).reshape(blocks, width), axis=1)
    rise = jnp.exp(log_gain)
    fall = jnp.exp(-log_gain)
    offsets = jnp.arange(width, dtype=jnp.float32)
    lag = offsets[:, None] - offsets[None, :]
    lower = lag >= 0.0
    lag_pos = jnp.where(lower, lag, 0.0)
    decay = jnp.exp(-damping[:, None, None] * lag_pos[None, :, :])
    turn = frequency[:, None, None] * lag_pos[None, :, :]
    kernel_re = jnp.where(lower[None, :, :], decay * jnp.cos(turn), 0.0)
    kernel_im = jnp.where(lower[None, :, :], decay * jnp.sin(turn), 0.0)
    pushed = (drive[:, None] * modal).reshape(owned, blocks, width) * fall[None, :, :]
    local_re = (
        jnp.einsum("mts,mns->mnt", kernel_re, pushed, precision=lax.Precision.HIGHEST)
        * rise[None, :, :]
    )
    local_im = (
        jnp.einsum("mts,mns->mnt", kernel_im, pushed, precision=lax.Precision.HIGHEST)
        * rise[None, :, :]
    )
    ahead = offsets + 1.0
    power_mag = jnp.exp(-damping[:, None] * ahead[None, :])
    power_re = power_mag * jnp.cos(frequency[:, None] * ahead[None, :])
    power_im = power_mag * jnp.sin(frequency[:, None] * ahead[None, :])
    carry_re_all = power_re[:, None, :] * rise[None, :, :]
    carry_im_all = power_im[:, None, :] * rise[None, :, :]
    unit = jnp.ones((owned,), jnp.float32)
    nothing = jnp.zeros((owned,), jnp.float32)
    running = (unit, nothing, nothing, nothing)
    entering = []
    for index in range(blocks):
        entering.append(running)
        piece = (
            carry_re_all[:, index, width - 1],
            carry_im_all[:, index, width - 1],
            local_re[:, index, width - 1],
            local_im[:, index, width - 1],
        )
        running = combine(running, piece)
    incoming = carried_in(running, "tm", combine, (unit, nothing, nothing, nothing))
    state_re = []
    state_im = []
    for index in range(blocks):
        joined = combine(incoming, entering[index])
        state_re.append(joined[2])
        state_im.append(joined[3])
    enter_re = jnp.stack(state_re, axis=1)
    enter_im = jnp.stack(state_im, axis=1)
    history = (
        carry_re_all * enter_re[:, :, None] - carry_im_all * enter_im[:, :, None] + local_re
    ).reshape(owned, steps)
    rounded = history.astype(jnp.bfloat16)
    block = shapes
    field = lax.dot_general(
        lax.all_gather(rounded, "dof", axis=0, tiled=True),
        block,
        (((0,), (0,)), ((), ())),
        preferred_element_type=jnp.float32,
    )
    return (field.astype(jnp.bfloat16), history)


def solution(mesh):
    placed = (P("tm", "dof"), P("dof", None), P("dof"), P("dof"), P("dof"), P("tm"), P(None, "dof"))
    part = functools.partial(fused, mesh.shape["tm"]) if mesh.shape["dof"] == 8 else body
    return jax.shard_map(
        part,
        mesh=mesh,
        in_specs=placed,
        out_specs=(P("tm", "dof"), P("dof", "tm")),
        check_vma=False,
    )
```

```python
import functools

import jax
import jax.numpy as jnp
from jax import lax
from jax.experimental import pallas as pl
from jax.experimental.pallas import tpu as pltpu
from jax.sharding import PartitionSpec as P

MESH = pl.DeviceIdType.MESH
NSUB = 2
SEGS = 8
CORE, DA, DB, XA, XB, YA, YB = 0, 4, 5, 6, 7, 8, 9
GXA, GXB, GYA, GYB, GP, FA, FB, PX, PY, PD, TM = 10, 11, 12, 13, 14, 15, 16, 17, 18, 19, 20


def cmul(ar, ai, br, bi):
    return ar * br - ai * bi, ar * bi + ai * br


def power(ar, ai, exponent):
    result = None
    while exponent:
        if exponent & 1:
            result = (ar, ai) if result is None else cmul(*result, ar, ai)
        exponent >>= 1
        if exponent:
            ar, ai = cmul(ar, ai, ar, ai)
    return result


def kernel(
    tms, damping, frequency, gains, index, loads_in, phi, shapes, field, hist,
    pars, onehot, spread, loads, row_loads, phi_buf, shapes_buf, tx_core, rx_core, own, tx_d, tx_x, tx_y, rx_d, rx_x, rx_y,
    mod, tx_tm, rx_tm, carry, gath, acc, turned, rounded,
    send, recv, loads_sem, phi_sem, shapes_sem, turned_sem, field_sem,
):
    steps = loads.shape[0]
    half = steps // 2
    owned = pars.shape[1]
    width = owned // NSUB
    cols = width // 128
    seg = steps // SEGS
    rows = phi.shape[0]
    channels = loads.shape[1]
    points = shapes.shape[1]
    tile = min(512, points)
    top, low = pl.ds(0, half), pl.ds(half, half)

    d = lax.axis_index("dof")
    me = lax.axis_index("tm")
    core = lax.rem(d, 2)
    px = lax.rem(d // 2, 2)
    py = d // 4
    other = 1 - core
    partner = d + 1 - 2 * core
    xn = d + 2 * (1 - 2 * px)
    yn = d + 4 * (1 - 2 * py)

    def owner(q, cc):
        fx, fy = q % 2, q // 2
        x = px + fx * (1 - 2 * px)
        y = py + fy * (1 - 2 * py)
        return (y * 2 + x) * 2 + cc

    def remote(src, dst, kind, s, to):
        return pltpu.make_async_remote_copy(
            src_ref=src, dst_ref=dst, send_sem=send.at[s, kind], recv_sem=recv.at[s, kind],
            device_id={"dof": to}, device_id_type=MESH,
        )

    def core_copy(q, s):
        return remote(tx_core.at[q, s], rx_core.at[q, s], CORE + q, s, partner)

    def piece(src, dst, span, kind, s, to):
        return remote(src.at[s, span], dst.at[s, span], kind, s, to)

    def da(s):
        return piece(tx_d, rx_d, top, DA, s, xn)

    def db(s):
        return piece(tx_d, rx_d, low, DB, s, yn)

    def xa(s):
        return piece(tx_x, rx_x, top, XA, s, xn)

    def xb(s):
        return piece(tx_x, rx_x, low, XB, s, xn)

    def ya(s):
        return piece(tx_y, rx_y, top, YA, s, yn)

    def yb(s):
        return piece(tx_y, rx_y, low, YB, s, yn)

    def lanes_of(q, r, s):
        return pl.ds(((s * 4 + q) * 2 + r) * width, width)

    def gathered(src, dst, span, kind, s, to):
        return remote(gath.at[span, lanes_of(*src, s)], gath.at[span, lanes_of(*dst, s)], kind, s, to)

    whole = pl.ds(0, steps)

    def gxa(s):
        return gathered((0, 0), (1, 0), top, GXA, s, xn)

    def gxb(s):
        return gathered((0, 0), (1, 0), low, GXB, s, xn)

    def gya(s):
        return gathered((0, 0), (2, 0), top, GYA, s, yn)

    def gyb(s):
        return gathered((0, 0), (2, 0), low, GYB, s, yn)

    def gp(s):
        return gathered((0, 0), (0, 1), whole, GP, s, partner)

    def fa(s):
        return gathered((1, 0), (3, 0), top, FA, s, yn)

    def fb(s):
        return gathered((2, 0), (3, 0), low, FB, s, xn)

    def pq(q, s):
        return gathered((q, 0), (q, 1), whole, PX + q - 1, s, partner)

    def state_copy(dk, s, to):
        return pltpu.make_async_remote_copy(
            src_ref=tx_tm.at[s], dst_ref=rx_tm.at[dk - 1, s],
            send_sem=send.at[s, TM + dk - 1], recv_sem=recv.at[s, TM + dk - 1],
            device_id={"tm": to}, device_id_type=MESH,
        )

    def phi_copy(q, r, s):
        start = pl.multiple_of(owner(q, other if r else core) * owned + s * width, width)
        return pltpu.make_async_copy(
            phi.at[:, pl.ds(start, width)], phi_buf.at[s, q, r], phi_sem.at[s, q, r]
        )

    def shapes_copy(q, r, s):
        start = pl.multiple_of(owner(q, other if r else core) * owned + s * width, width)
        return pltpu.make_async_copy(
            shapes.at[pl.ds(start, width), :], shapes_buf.at[lanes_of(q, r, s), :], shapes_sem.at[s, q, r]
        )

    loads_copy = pltpu.make_async_copy(loads_in, loads, loads_sem)
    order = (3, 1, 2, 0)

    barrier = pltpu.get_barrier_semaphore()
    for to in (partner, xn, yn):
        pl.semaphore_signal(barrier, inc=1, device_id={"dof": to}, device_id_type=MESH)
    for dk in range(1, tms):
        to = lax.rem(me + dk, tms)
        pl.semaphore_signal(barrier, inc=1, device_id={"tm": to}, device_id_type=MESH)
    loads_copy.start()
    for s in range(NSUB):
        for q in order:
            phi_copy(q, 1, s).start()
            phi_copy(q, 0, s).start()

    names = jnp.broadcast_to(index[...] - d * rows, (128, channels)).T
    for j in range(rows // 128):
        place = lax.broadcasted_iota(jnp.int32, (channels, 128), 1) + j * 128
        onehot[:, j * 128:(j + 1) * 128] = jnp.where(place == names, 1.0, 0.0).astype(jnp.bfloat16)
    loads_copy.wait()
    row_loads[...] = jnp.dot(loads[...], onehot[...], preferred_element_type=jnp.float32).astype(jnp.bfloat16)

    def partial_modal(q, r, s):
        phi_copy(q, r, s).wait()
        return jnp.dot(row_loads[...], phi_buf[s, q, r], preferred_element_type=jnp.float32)

    def for_partner(q, s):
        tx_core[q, s] = partial_modal(q, 1, s).astype(jnp.bfloat16)
        if q == order[0] and s == 0:
            pl.semaphore_wait(barrier, 3 + tms - 1)
        core_copy(q, s).start()

    def chip_sum(q, s, span):
        return own[s, q, span] + rx_core[q, s, span].astype(jnp.float32)

    def to_chip(q, s):
        core_copy(q, s).wait_recv()
        if q == 3:
            tx_d[s] = chip_sum(q, s, pl.ds(0, steps)).astype(jnp.bfloat16)
            da(s).start()
            db(s).start()
        if q == 1:
            tx_x[s, top] = chip_sum(q, s, top).astype(jnp.bfloat16)
            xa(s).start()
        if q == 2:
            tx_y[s, low] = chip_sum(q, s, low).astype(jnp.bfloat16)
            yb(s).start()

    def partials(s, between=None):
        for n, q in enumerate(order):
            for_partner(q, s)
            if n:
                to_chip(order[n - 1], s)
            if between is not None and n == 2:
                between()
            own[s, q] = partial_modal(q, 0, s)

    def parameters():
        x = 2.0 * damping[...]
        series = jnp.ones_like(x)
        for n in range(12, 1, -1):
            series = 1.0 - x * series / n
        drive = jnp.sqrt(jnp.where(x < 0.5, x * series, 1.0 - jnp.exp(-x)))
        radius = jnp.exp(-damping[...])
        pars[0:1, :] = radius * jnp.cos(frequency[...])
        pars[1:2, :] = radius * jnp.sin(frequency[...])
        pars[2:3, :] = drive
        spread[...] = jnp.broadcast_to(gains[...].reshape(1, steps), (128, steps)).T

    def pass_on(s):
        db(s).wait_recv()
        tx_x[s, low] = (chip_sum(1, s, low) + rx_d[s, low].astype(jnp.float32)).astype(jnp.bfloat16)
        xb(s).start()
        da(s).wait_recv()
        tx_y[s, top] = (chip_sum(2, s, top) + rx_d[s, top].astype(jnp.float32)).astype(jnp.bfloat16)
        ya(s).start()

    def par(s, j):
        lanes = slice(s * width + j * 128, s * width + (j + 1) * 128)
        return pars[0:1, lanes], pars[1:2, lanes], pars[2:3, lanes]

    def scan(s, start, store):
        coefs = [tuple(jnp.broadcast_to(v, (SEGS, 128)) for v in par(s, j)[:2]) for j in range(cols)]

        def step(i, state):
            total, waves = state
            at = pl.ds(i, SEGS, stride=seg)
            gain = spread[at, :]
            out = []
            for j in range(cols):
                re, im = cmul(*coefs[j], *waves[j])
                re = gain * re + mod[s, j, at, :]
                im = gain * im
                if store:
                    mod[s, j, at, :] = re
                out.append((re, im))
            return total * gain, tuple(out)

        one = jnp.ones((SEGS, 128), jnp.float32)
        return lax.fori_loop(0, seg, step, (one, tuple(start)), unroll=8)

    def local_states(s):
        for copy in (core_copy(0, s), xa(s), xb(s), ya(s), yb(s)):
            copy.wait_recv()
        for j in range(cols):
            lanes = slice(j * 128, (j + 1) * 128)
            value = own[s, 0, :, lanes]
            for part in (rx_core.at[0], rx_x, rx_y):
                value += part[s, :, lanes].astype(jnp.float32)
            mod[s, j] = value * par(s, j)[2]
        zero = jnp.zeros((SEGS, 128), jnp.float32)
        total, ends = scan(s, [(zero, zero)] * cols, False)
        kept = []
        for j in range(cols):
            lanes = slice(j * 128, (j + 1) * 128)
            a, b, _ = par(s, j)
            ar, ai = power(a, b, seg)
            state = (jnp.zeros((1, 128), jnp.float32),) * 2
            prod = (jnp.ones((1, 128), jnp.float32), jnp.zeros((1, 128), jnp.float32))
            entering, products = [], []
            gain = jnp.ones((1, 128), jnp.float32)
            for k in range(SEGS):
                entering.append(state)
                products.append(prod)
                g = total[k:k + 1]
                c = (ar * g, ai * g)
                moved = cmul(*c, *state)
                state = (moved[0] + ends[j][0][k:k + 1], moved[1] + ends[j][1][k:k + 1])
                prod = cmul(*c, *prod)
                gain = gain * g
            tx_tm[s, 0:1, lanes] = state[0]
            tx_tm[s, 1:2, lanes] = state[1]
            tx_tm[s, 2:3, lanes] = gain
            kept.append(tuple(
                jnp.concatenate([v[n] for v in some], axis=0) for some in (entering, products) for n in (0, 1)
            ))
        for dk in range(1, tms):
            @pl.when(me + dk < tms)
            def _():
                state_copy(dk, s, me + dk).start()
        return kept

    def finish(s, kept):
        carry[s] = jnp.zeros(carry.shape[1:], jnp.float32)
        for dk in range(tms - 1, 0, -1):
            @pl.when(me >= dk)
            def _():
                state_copy(dk, s, me).wait_recv()
                for j in range(cols):
                    lanes = slice(j * 128, (j + 1) * 128)
                    a, b, _ = par(s, j)
                    ar, ai = power(a, b, steps)
                    gain = rx_tm[dk - 1, s, 2:3, lanes]
                    re, im = cmul(ar * gain, ai * gain, carry[s, 0:1, lanes], carry[s, 1:2, lanes])
                    carry[s, 0:1, lanes] = re + rx_tm[dk - 1, s, 0:1, lanes]
                    carry[s, 1:2, lanes] = im + rx_tm[dk - 1, s, 1:2, lanes]
        start = []
        for j in range(cols):
            lanes = slice(j * 128, (j + 1) * 128)
            er, ei, kr, ki = kept[j]
            re, im = cmul(kr, ki, carry[s, 0:1, lanes], carry[s, 1:2, lanes])
            start.append((er + re, ei + im))
        scan(s, start, True)
        for j in range(cols):
            gath[:, pl.ds(s * 8 * width + j * 128, 128)] = mod[s, j].astype(jnp.bfloat16)
        for copy in (gxa(s), gyb(s), gp(s), gxb(s), gya(s)):
            copy.start()
        for j in range(cols):
            turned[s * width + j * 128:s * width + (j + 1) * 128, :] = mod[s, j].T
        turned_copy(s).start()

    def turned_copy(s):
        at = pl.ds(s * width, width)
        return pltpu.make_async_copy(turned.at[at], hist.at[at], turned_sem.at[s])

    def forward(s):
        gxa(s).wait_recv()
        fa(s).start()
        gyb(s).wait_recv()
        fb(s).start()

    def share(s):
        gxb(s).wait_recv()
        pq(1, s).start()
        gya(s).wait_recv()
        pq(2, s).start()

    def share_last(s):
        fa(s).wait_recv()
        fb(s).wait_recv()
        pq(3, s).start()

    def field_copy(n):
        at = pl.ds(pl.multiple_of(n * tile, tile), tile)
        return pltpu.make_async_copy(rounded.at[:, at], field.at[:, at], field_sem.at[n])

    def expand(first, count, mode):
        for block in range(first, first + count):
            s, q = block // 4, block % 4
            shapes_copy(q, 0, s).wait()
            shapes_copy(q, 1, s).wait()
        deep = pl.ds(first * 2 * width, count * 2 * width)

        def one(n, _):
            at = pl.ds(pl.multiple_of(n * tile, tile), tile)
            value = jnp.dot(gath[:, deep], shapes_buf[deep, at], preferred_element_type=jnp.float32)
            if mode != "first":
                value += acc[:, at]
            if mode == "last":
                rounded[:, at] = value.astype(jnp.bfloat16)
                field_copy(n).start()
            else:
                acc[:, at] = value
            return 0

        lax.fori_loop(0, points // tile, one, 0)

    partials(0)
    for s in range(NSUB):
        for q in range(4):
            shapes_copy(q, 0, s).start()
            shapes_copy(q, 1, s).start()
    parameters()
    partials(1, lambda: pass_on(0))
    kept_0 = local_states(0)
    pass_on(1)
    finish(0, kept_0)
    kept_1 = local_states(1)
    gp(0).wait_recv()
    expand(0, 1, "first")
    forward(0)
    finish(1, kept_1)
    share(0)
    share_last(0)
    pq(1, 0).wait_recv()
    pq(2, 0).wait_recv()
    expand(1, 2, "add")
    forward(1)
    pq(3, 0).wait_recv()
    gp(1).wait_recv()
    expand(3, 2, "add")
    share(1)
    share_last(1)
    pq(1, 1).wait_recv()
    pq(2, 1).wait_recv()
    expand(5, 2, "add")
    pq(3, 1).wait_recv()
    expand(7, 1, "last")

    for n in range(points // tile):
        field_copy(n).wait()
    for s in range(NSUB):
        turned_copy(s).wait()
    for s in range(NSUB):
        for q in range(4):
            core_copy(q, s).wait_send()
        for copy in (
            da(s), db(s), xa(s), xb(s), ya(s), yb(s), gxa(s), gxb(s), gya(s), gyb(s), gp(s), fa(s), fb(s),
            pq(1, s), pq(2, s), pq(3, s),
        ):
            copy.wait_send()
        for dk in range(1, tms):
            @pl.when(me + dk < tms)
            def _():
                state_copy(dk, s, me).wait_send()


def hand_over(*arrays):
    pieces = 4

    def copies(*refs):
        count = len(arrays)
        sources, targets, held, (into, out) = refs[:count], refs[count:2 * count], refs[2 * count:3 * count], refs[3 * count:]
        pairs = []
        for n in range(count):
            rows = arrays[n].shape[0] // pieces
            for piece in range(pieces):
                at = pl.ds(piece * rows, rows)
                pairs.append((
                    pltpu.make_async_copy(sources[n].at[at], held[n].at[at], into.at[n, piece]),
                    pltpu.make_async_copy(held[n].at[at], targets[n].at[at], out.at[n, piece]),
                ))
        for first, _ in pairs:
            first.start()
        for first, second in pairs:
            first.wait()
            second.start()
        for _, second in pairs:
            second.wait()

    place = pl.BlockSpec(memory_space=pltpu.HBM)
    return pl.pallas_call(
        copies,
        out_shape=tuple(jax.ShapeDtypeStruct(a.shape, a.dtype) for a in arrays),
        in_specs=[place] * len(arrays),
        out_specs=(place,) * len(arrays),
        scratch_shapes=[pltpu.VMEM(a.shape, a.dtype) for a in arrays]
        + [pltpu.SemaphoreType.DMA((len(arrays), pieces))] * 2,
        compiler_params=pltpu.CompilerParams(vmem_limit_bytes=16 * 1024 * 1024),
        cost_estimate=pl.CostEstimate(
            flops=0, bytes_accessed=sum(2 * a.size * a.dtype.itemsize for a in arrays), transcendentals=0
        ),
    )(*arrays)


def fused(tms, loads, phi, load_index, damping, frequency, gains, shapes):
    owned, steps, channels = damping.shape[0], loads.shape[0], loads.shape[1]
    rows, points, modes = phi.shape[0], shapes.shape[1], shapes.shape[0]
    width = owned // NSUB
    b16, f32 = jnp.bfloat16, jnp.float32
    kinds = TM + tms - 1
    small = pl.BlockSpec(memory_space=pltpu.VMEM)
    large = pl.BlockSpec(memory_space=pl.ANY)
    results = pl.pallas_call(
        functools.partial(kernel, tms),
        out_shape=(
            jax.ShapeDtypeStruct((steps, points), b16),
            jax.ShapeDtypeStruct((owned, steps), f32),
        ),
        in_specs=[small, small, small, small, large, large, large],
        out_specs=(large, large),
        scratch_shapes=[
            pltpu.VMEM((8, owned), f32),
            pltpu.VMEM((channels, rows), b16),
            pltpu.VMEM((steps, 128), f32),
            pltpu.VMEM((steps, channels), b16),
            pltpu.VMEM((steps, rows), b16),
            pltpu.VMEM((NSUB, 4, 2, rows, width), b16),
            pltpu.VMEM((modes, points), b16),
            pltpu.VMEM((4, NSUB, steps, width), b16),
            pltpu.VMEM((4, NSUB, steps, width), b16),
            pltpu.VMEM((NSUB, 4, steps, width), f32),
        ] + [pltpu.VMEM((NSUB, steps, width), b16)] * 6 + [
            pltpu.VMEM((NSUB, width // 128, steps, 128), f32),
            pltpu.VMEM((NSUB, 8, width), f32),
            pltpu.VMEM((tms - 1, NSUB, 8, width), f32),
            pltpu.VMEM((NSUB, 8, width), f32),
            pltpu.VMEM((steps, modes), b16),
            pltpu.VMEM((steps, points), f32),
            pltpu.VMEM((owned, steps), f32),
            pltpu.VMEM((steps, points), b16),
            pltpu.SemaphoreType.DMA((NSUB, kinds)),
            pltpu.SemaphoreType.DMA((NSUB, kinds)),
            pltpu.SemaphoreType.DMA,
            pltpu.SemaphoreType.DMA((NSUB, 4, 2)),
            pltpu.SemaphoreType.DMA((NSUB, 4, 2)),
            pltpu.SemaphoreType.DMA((NSUB,)),
            pltpu.SemaphoreType.DMA((points // min(512, points),)),
        ],
        compiler_params=pltpu.CompilerParams(
            collective_id=0, has_side_effects=True, vmem_limit_bytes=56 * 1024 * 1024
        ),
        cost_estimate=pl.CostEstimate(
            flops=2 * steps * (modes * (points + rows) + channels * rows),
            bytes_accessed=2 * (modes * points + rows * modes + steps * points),
            transcendentals=0,
        ),
    )(damping.reshape(1, owned), frequency.reshape(1, owned), gains, load_index.reshape(1, channels), loads, phi, shapes)
    return hand_over(*results)


def carried_in(value, axis, join, neutral):
    count, mine = (lax.axis_size(axis), lax.axis_index(axis))
    pieces = jax.tree.map(lambda part: lax.all_gather(part, axis), value)
    subtotal = jax.tree.map(
        lambda part, zero: jnp.full_like(part, 0) + jnp.asarray(zero, part.dtype), value, neutral
    )

    def step(position, subtotal):
        longer = join(subtotal, jax.tree.map(lambda part: part[position], pieces))
        return jax.tree.map(lambda new, old: jnp.where(position < mine, new, old), longer, subtotal)

    return lax.fori_loop(0, count - 1, step, subtotal)


def combine(earlier, later):
    ear, eai, ebr, ebi = earlier
    lar, lai, lbr, lbi = later
    return (
        lar * ear - lai * eai,
        lar * eai + lai * ear,
        lar * ebr - lai * ebi + lbr,
        lar * ebi + lai * ebr + lbi,
    )


def body(loads, phi, load_index, damping, frequency, gains, shapes):
    owned = damping.shape[0]
    steps = loads.shape[0]
    rows_here = phi.shape[0]
    local_index = load_index - lax.axis_index("dof") * rows_here
    selected = jnp.take(phi, local_index, axis=0)
    columns = lax.all_to_all(selected, "dof", split_axis=1, concat_axis=0, tiled=True)
    block = columns
    modal = lax.dot_general(
        block,
        lax.all_gather(loads, "dof", axis=1, tiled=True),
        (((0,), (1,)), ((), ())),
        preferred_element_type=jnp.float32,
    )
    drive = jnp.sqrt(-jnp.expm1(-2.0 * damping))
    width = min(128, steps)
    blocks = steps // width
    log_gain = jnp.cumsum(jnp.log(gains).reshape(blocks, width), axis=1)
    rise = jnp.exp(log_gain)
    fall = jnp.exp(-log_gain)
    offsets = jnp.arange(width, dtype=jnp.float32)
    lag = offsets[:, None] - offsets[None, :]
    lower = lag >= 0.0
    lag_pos = jnp.where(lower, lag, 0.0)
    decay = jnp.exp(-damping[:, None, None] * lag_pos[None, :, :])
    turn = frequency[:, None, None] * lag_pos[None, :, :]
    kernel_re = jnp.where(lower[None, :, :], decay * jnp.cos(turn), 0.0)
    kernel_im = jnp.where(lower[None, :, :], decay * jnp.sin(turn), 0.0)
    pushed = (drive[:, None] * modal).reshape(owned, blocks, width) * fall[None, :, :]
    local_re = (
        jnp.einsum("mts,mns->mnt", kernel_re, pushed, precision=lax.Precision.HIGHEST)
        * rise[None, :, :]
    )
    local_im = (
        jnp.einsum("mts,mns->mnt", kernel_im, pushed, precision=lax.Precision.HIGHEST)
        * rise[None, :, :]
    )
    ahead = offsets + 1.0
    power_mag = jnp.exp(-damping[:, None] * ahead[None, :])
    power_re = power_mag * jnp.cos(frequency[:, None] * ahead[None, :])
    power_im = power_mag * jnp.sin(frequency[:, None] * ahead[None, :])
    carry_re_all = power_re[:, None, :] * rise[None, :, :]
    carry_im_all = power_im[:, None, :] * rise[None, :, :]
    unit = jnp.ones((owned,), jnp.float32)
    nothing = jnp.zeros((owned,), jnp.float32)
    running = (unit, nothing, nothing, nothing)
    entering = []
    for index in range(blocks):
        entering.append(running)
        piece = (
            carry_re_all[:, index, width - 1],
            carry_im_all[:, index, width - 1],
            local_re[:, index, width - 1],
            local_im[:, index, width - 1],
        )
        running = combine(running, piece)
    incoming = carried_in(running, "tm", combine, (unit, nothing, nothing, nothing))
    state_re = []
    state_im = []
    for index in range(blocks):
        joined = combine(incoming, entering[index])
        state_re.append(joined[2])
        state_im.append(joined[3])
    enter_re = jnp.stack(state_re, axis=1)
    enter_im = jnp.stack(state_im, axis=1)
    history = (
        carry_re_all * enter_re[:, :, None] - carry_im_all * enter_im[:, :, None] + local_re
    ).reshape(owned, steps)
    rounded = history.astype(jnp.bfloat16)
    block = shapes
    field = lax.dot_general(
        lax.all_gather(rounded, "dof", axis=0, tiled=True),
        block,
        (((0,), (0,)), ((), ())),
        preferred_element_type=jnp.float32,
    )
    return (field.astype(jnp.bfloat16), history)


def solution(mesh):
    placed = (P("tm", "dof"), P("dof", None), P("dof"), P("dof"), P("dof"), P("tm"), P(None, "dof"))
    part = functools.partial(fused, mesh.shape["tm"]) if mesh.shape["dof"] == 8 else body
    return jax.shard_map(
        part,
        mesh=mesh,
        in_specs=placed,
        out_specs=(P("tm", "dof"), P("dof", "tm")),
        check_vma=False,
    )
```

```python
import functools

import jax
import jax.numpy as jnp
from jax import lax
from jax.experimental import pallas as pl
from jax.experimental.pallas import tpu as pltpu
from jax.sharding import PartitionSpec as P

MESH = pl.DeviceIdType.MESH
NSUB = 2
BLOCKS = ((0, 0), (0, 1), (1, 0), (2, 0), (1, 1), (2, 1), (3, 0), (3, 1))
SEGS = 8
CORE, DA, DB, XA, XB, YA, YB = 0, 4, 5, 6, 7, 8, 9
GXA, GXB, GYA, GYB, GP, FA, FB, PX, PY, PD, TM = 10, 11, 12, 13, 14, 15, 16, 17, 18, 19, 20


def cmul(ar, ai, br, bi):
    return ar * br - ai * bi, ar * bi + ai * br


def power(ar, ai, exponent):
    result = None
    while exponent:
        if exponent & 1:
            result = (ar, ai) if result is None else cmul(*result, ar, ai)
        exponent >>= 1
        if exponent:
            ar, ai = cmul(ar, ai, ar, ai)
    return result


def kernel(
    tms, damping, frequency, gains, index, loads, phi, shapes, field, hist,
    pars, onehot, spread, row_loads, phi_buf, shapes_buf, tx_core, rx_core, own, tx_d, tx_x, tx_y, rx_d, rx_x, rx_y,
    mod, tx_tm, rx_tm, carry, gath, acc,
    send, recv, phi_sem, shapes_sem,
):
    steps = loads.shape[0]
    half = steps // 2
    owned = pars.shape[1]
    width = owned // NSUB
    cols = width // 128
    seg = steps // SEGS
    rows = phi.shape[0]
    channels = loads.shape[1]
    points = shapes.shape[1]
    tile = min(512, points)
    top, low = pl.ds(0, half), pl.ds(half, half)

    d = lax.axis_index("dof")
    me = lax.axis_index("tm")
    core = lax.rem(d, 2)
    px = lax.rem(d // 2, 2)
    py = d // 4
    other = 1 - core
    partner = d + 1 - 2 * core
    xn = d + 2 * (1 - 2 * px)
    yn = d + 4 * (1 - 2 * py)

    def owner(q, cc):
        fx, fy = q % 2, q // 2
        x = px + fx * (1 - 2 * px)
        y = py + fy * (1 - 2 * py)
        return (y * 2 + x) * 2 + cc

    def remote(src, dst, kind, s, to):
        return pltpu.make_async_remote_copy(
            src_ref=src, dst_ref=dst, send_sem=send.at[s, kind], recv_sem=recv.at[s, kind],
            device_id={"dof": to}, device_id_type=MESH,
        )

    def core_copy(q, s):
        return remote(tx_core.at[q, s], rx_core.at[q, s], CORE + q, s, partner)

    def piece(src, dst, span, kind, s, to):
        return remote(src.at[s, span], dst.at[s, span], kind, s, to)

    def da(s):
        return piece(tx_d, rx_d, top, DA, s, xn)

    def db(s):
        return piece(tx_d, rx_d, low, DB, s, yn)

    def xa(s):
        return piece(tx_x, rx_x, top, XA, s, xn)

    def xb(s):
        return piece(tx_x, rx_x, low, XB, s, xn)

    def ya(s):
        return piece(tx_y, rx_y, top, YA, s, yn)

    def yb(s):
        return piece(tx_y, rx_y, low, YB, s, yn)

    def lanes_of(q, r, s):
        return pl.ds((s * 8 + BLOCKS.index((q, r))) * width, width)

    def gathered(src, dst, span, kind, s, to):
        return remote(gath.at[span, lanes_of(*src, s)], gath.at[span, lanes_of(*dst, s)], kind, s, to)

    whole = pl.ds(0, steps)

    def gxa(s):
        return gathered((0, 0), (1, 0), top, GXA, s, xn)

    def gxb(s):
        return gathered((0, 0), (1, 0), low, GXB, s, xn)

    def gya(s):
        return gathered((0, 0), (2, 0), top, GYA, s, yn)

    def gyb(s):
        return gathered((0, 0), (2, 0), low, GYB, s, yn)

    def gp(s):
        return gathered((0, 0), (0, 1), whole, GP, s, partner)

    def fa(s):
        return gathered((1, 0), (3, 0), top, FA, s, yn)

    def fb(s):
        return gathered((2, 0), (3, 0), low, FB, s, xn)

    def pq(q, s):
        return gathered((q, 0), (q, 1), whole, PX + q - 1, s, partner)

    def state_copy(dk, s, to):
        return pltpu.make_async_remote_copy(
            src_ref=tx_tm.at[s], dst_ref=rx_tm.at[dk - 1, s],
            send_sem=send.at[s, TM + dk - 1], recv_sem=recv.at[s, TM + dk - 1],
            device_id={"tm": to}, device_id_type=MESH,
        )

    def phi_copy(q, r, s):
        start = pl.multiple_of(owner(q, other if r else core) * owned + s * width, width)
        return pltpu.make_async_copy(
            phi.at[:, pl.ds(start, width)], phi_buf.at[s, q, r], phi_sem.at[s, q, r]
        )

    def shapes_copy(q, r, s):
        start = pl.multiple_of(owner(q, other if r else core) * owned + s * width, width)
        return pltpu.make_async_copy(
            shapes.at[pl.ds(start, width), :], shapes_buf.at[lanes_of(q, r, s), :], shapes_sem.at[s, q, r]
        )

    order = (3, 1, 2, 0)

    barrier = pltpu.get_barrier_semaphore()
    for to in (partner, xn, yn):
        pl.semaphore_signal(barrier, inc=1, device_id={"dof": to}, device_id_type=MESH)
    for dk in range(1, tms):
        to = lax.rem(me + dk, tms)
        pl.semaphore_signal(barrier, inc=1, device_id={"tm": to}, device_id_type=MESH)
    def start_phi(s):
        for q in order:
            phi_copy(q, 1, s).start()
            phi_copy(q, 0, s).start()

    start_phi(0)

    names = jnp.broadcast_to(index[...] - d * rows, (128, channels)).T
    for j in range(rows // 128):
        place = lax.broadcasted_iota(jnp.int32, (channels, 128), 1) + j * 128
        onehot[:, j * 128:(j + 1) * 128] = jnp.where(place == names, 1.0, 0.0).astype(jnp.bfloat16)
    row_loads[...] = jnp.dot(loads[...], onehot[...], preferred_element_type=jnp.float32).astype(jnp.bfloat16)

    def partial_modal(q, r, s):
        phi_copy(q, r, s).wait()
        return jnp.dot(row_loads[...], phi_buf[s, q, r], preferred_element_type=jnp.float32)

    def for_partner(q, s):
        tx_core[q, s] = partial_modal(q, 1, s).astype(jnp.bfloat16)
        if q == order[0] and s == 0:
            start_phi(1)
            pl.semaphore_wait(barrier, 3 + tms - 1)
        core_copy(q, s).start()

    def chip_sum(q, s, span):
        return own[s, q, span] + rx_core[q, s, span].astype(jnp.float32)

    def to_chip(q, s):
        core_copy(q, s).wait_recv()
        if q == 3:
            tx_d[s] = chip_sum(q, s, pl.ds(0, steps)).astype(jnp.bfloat16)
            da(s).start()
            db(s).start()
        if q == 1:
            tx_x[s, top] = chip_sum(q, s, top).astype(jnp.bfloat16)
            xa(s).start()
        if q == 2:
            tx_y[s, low] = chip_sum(q, s, low).astype(jnp.bfloat16)
            yb(s).start()

    def partials(s, between=None):
        for n, q in enumerate(order):
            for_partner(q, s)
            if n:
                to_chip(order[n - 1], s)
            if between is not None and n == 2:
                between()
            own[s, q] = partial_modal(q, 0, s)

    def parameters():
        x = 2.0 * damping[...]
        series = jnp.ones_like(x)
        for n in range(12, 1, -1):
            series = 1.0 - x * series / n
        drive = jnp.sqrt(jnp.where(x < 0.5, x * series, 1.0 - jnp.exp(-x)))
        radius = jnp.exp(-damping[...])
        pars[0:1, :] = radius * jnp.cos(frequency[...])
        pars[1:2, :] = radius * jnp.sin(frequency[...])
        pars[2:3, :] = drive
        spread[...] = jnp.broadcast_to(gains[...].reshape(1, steps), (128, steps)).T

    def pass_on(s):
        db(s).wait_recv()
        tx_x[s, low] = (chip_sum(1, s, low) + rx_d[s, low].astype(jnp.float32)).astype(jnp.bfloat16)
        xb(s).start()
        da(s).wait_recv()
        tx_y[s, top] = (chip_sum(2, s, top) + rx_d[s, top].astype(jnp.float32)).astype(jnp.bfloat16)
        ya(s).start()

    def par(s, j):
        lanes = slice(s * width + j * 128, s * width + (j + 1) * 128)
        return pars[0:1, lanes], pars[1:2, lanes], pars[2:3, lanes]

    def scan(s, start, store):
        coefs = [tuple(jnp.broadcast_to(v, (SEGS, 128)) for v in par(s, j)[:2]) for j in range(cols)]

        def step(i, state):
            total, waves = state
            at = pl.ds(i, SEGS, stride=seg)
            gain = spread[at, :]
            out = []
            for j in range(cols):
                re, im = cmul(*coefs[j], *waves[j])
                re = gain * re + mod[s, j, at, :]
                im = gain * im
                if store:
                    mod[s, j, at, :] = re
                out.append((re, im))
            return total * gain, tuple(out)

        one = jnp.ones((SEGS, 128), jnp.float32)
        return lax.fori_loop(0, seg, step, (one, tuple(start)), unroll=8)

    def local_states(s):
        for copy in (core_copy(0, s), xa(s), xb(s), ya(s), yb(s)):
            copy.wait_recv()
        for j in range(cols):
            lanes = slice(j * 128, (j + 1) * 128)
            value = own[s, 0, :, lanes]
            for part in (rx_core.at[0], rx_x, rx_y):
                value += part[s, :, lanes].astype(jnp.float32)
            mod[s, j] = value * par(s, j)[2]
        zero = jnp.zeros((SEGS, 128), jnp.float32)
        total, ends = scan(s, [(zero, zero)] * cols, False)
        kept = []
        for j in range(cols):
            lanes = slice(j * 128, (j + 1) * 128)
            a, b, _ = par(s, j)
            ar, ai = power(a, b, seg)
            state = (jnp.zeros((1, 128), jnp.float32),) * 2
            prod = (jnp.ones((1, 128), jnp.float32), jnp.zeros((1, 128), jnp.float32))
            entering, products = [], []
            gain = jnp.ones((1, 128), jnp.float32)
            for k in range(SEGS):
                entering.append(state)
                products.append(prod)
                g = total[k:k + 1]
                c = (ar * g, ai * g)
                moved = cmul(*c, *state)
                state = (moved[0] + ends[j][0][k:k + 1], moved[1] + ends[j][1][k:k + 1])
                prod = cmul(*c, *prod)
                gain = gain * g
            tx_tm[s, 0:1, lanes] = state[0]
            tx_tm[s, 1:2, lanes] = state[1]
            tx_tm[s, 2:3, lanes] = gain
            kept.append(tuple(
                jnp.concatenate([v[n] for v in some], axis=0) for some in (entering, products) for n in (0, 1)
            ))
        for dk in range(1, tms):
            @pl.when(me + dk < tms)
            def _():
                state_copy(dk, s, me + dk).start()
        return kept

    def finish(s, kept):
        carry[s] = jnp.zeros(carry.shape[1:], jnp.float32)
        for dk in range(tms - 1, 0, -1):
            @pl.when(me >= dk)
            def _():
                state_copy(dk, s, me).wait_recv()
                for j in range(cols):
                    lanes = slice(j * 128, (j + 1) * 128)
                    a, b, _ = par(s, j)
                    ar, ai = power(a, b, steps)
                    gain = rx_tm[dk - 1, s, 2:3, lanes]
                    re, im = cmul(ar * gain, ai * gain, carry[s, 0:1, lanes], carry[s, 1:2, lanes])
                    carry[s, 0:1, lanes] = re + rx_tm[dk - 1, s, 0:1, lanes]
                    carry[s, 1:2, lanes] = im + rx_tm[dk - 1, s, 1:2, lanes]
        start = []
        for j in range(cols):
            lanes = slice(j * 128, (j + 1) * 128)
            er, ei, kr, ki = kept[j]
            re, im = cmul(kr, ki, carry[s, 0:1, lanes], carry[s, 1:2, lanes])
            start.append((er + re, ei + im))
        scan(s, start, True)
        for j in range(cols):
            gath[:, pl.ds(s * 8 * width + j * 128, 128)] = mod[s, j].astype(jnp.bfloat16)
        for copy in (gxa(s), gyb(s), gp(s), gxb(s), gya(s)):
            copy.start()
        for j in range(cols):
            hist[s * width + j * 128:s * width + (j + 1) * 128, :] = mod[s, j].T

    def forward(s):
        gxa(s).wait_recv()
        fa(s).start()
        gyb(s).wait_recv()
        fb(s).start()

    def share(s):
        gxb(s).wait_recv()
        pq(1, s).start()
        gya(s).wait_recv()
        pq(2, s).start()

    def share_last(s):
        fa(s).wait_recv()
        fb(s).wait_recv()
        pq(3, s).start()

    def expand(first, count, mode):
        for block in range(first, first + count):
            shapes_copy(*BLOCKS[block % 8], block // 8).wait()
        deep = pl.ds(first * width, count * width)

        def one(n, _):
            at = pl.ds(pl.multiple_of(n * tile, tile), tile)
            value = jnp.dot(gath[:, deep], shapes_buf[deep, at], preferred_element_type=jnp.float32)
            if mode != "first":
                value += acc[:, at]
            if mode == "last":
                field[:, at] = value.astype(jnp.bfloat16)
            else:
                acc[:, at] = value
            return 0

        lax.fori_loop(0, points // tile, one, 0)

    partials(0)
    for s in range(NSUB):
        for q, r in BLOCKS:
            shapes_copy(q, r, s).start()
    parameters()
    partials(1, lambda: pass_on(0))
    kept_0 = local_states(0)
    pass_on(1)
    finish(0, kept_0)
    kept_1 = local_states(1)
    gp(0).wait_recv()
    expand(0, 2, "first")
    forward(0)
    finish(1, kept_1)
    share(0)
    expand(2, 2, "add")
    share_last(0)
    pq(1, 0).wait_recv()
    pq(2, 0).wait_recv()
    expand(4, 2, "add")
    forward(1)
    pq(3, 0).wait_recv()
    gp(1).wait_recv()
    expand(6, 4, "add")
    share(1)
    expand(10, 2, "add")
    pq(1, 1).wait_recv()
    pq(2, 1).wait_recv()
    expand(12, 2, "add")
    share_last(1)
    expand(14, 1, "add")
    pq(3, 1).wait_recv()
    expand(15, 1, "last")

    for s in range(NSUB):
        for q in range(4):
            core_copy(q, s).wait_send()
        for copy in (
            da(s), db(s), xa(s), xb(s), ya(s), yb(s), gxa(s), gxb(s), gya(s), gyb(s), gp(s), fa(s), fb(s),
            pq(1, s), pq(2, s), pq(3, s),
        ):
            copy.wait_send()
        for dk in range(1, tms):
            @pl.when(me + dk < tms)
            def _():
                state_copy(dk, s, me).wait_send()


def hand_over(*arrays):
    pieces = 4

    def copies(*refs):
        count = len(arrays)
        started = []
        for n in range(count):
            rows = arrays[n].shape[0] // pieces
            for piece in range(pieces):
                at = pl.ds(piece * rows, rows)
                started.append(
                    pltpu.make_async_copy(refs[n].at[at], refs[count + n].at[at], refs[2 * count].at[n, piece])
                )
        for copy in started:
            copy.start()
        for copy in started:
            copy.wait()

    return pl.pallas_call(
        copies,
        out_shape=tuple(jax.ShapeDtypeStruct(a.shape, a.dtype) for a in arrays),
        in_specs=[pl.BlockSpec(memory_space=pltpu.VMEM)] * len(arrays),
        out_specs=(pl.BlockSpec(memory_space=pltpu.HBM),) * len(arrays),
        scratch_shapes=[pltpu.SemaphoreType.DMA((len(arrays), pieces))],
        compiler_params=pltpu.CompilerParams(vmem_limit_bytes=16 * 1024 * 1024),
        cost_estimate=pl.CostEstimate(
            flops=0, bytes_accessed=sum(2 * a.size * a.dtype.itemsize for a in arrays), transcendentals=0
        ),
    )(*arrays)


def fused(tms, loads, phi, load_index, damping, frequency, gains, shapes):
    owned, steps, channels = damping.shape[0], loads.shape[0], loads.shape[1]
    rows, points, modes = phi.shape[0], shapes.shape[1], shapes.shape[0]
    width = owned // NSUB
    b16, f32 = jnp.bfloat16, jnp.float32
    kinds = TM + tms - 1
    small = pl.BlockSpec(memory_space=pltpu.VMEM)
    large = pl.BlockSpec(memory_space=pltpu.HBM)
    results = pl.pallas_call(
        functools.partial(kernel, tms),
        out_shape=(
            jax.ShapeDtypeStruct((steps, points), b16),
            jax.ShapeDtypeStruct((owned, steps), f32),
        ),
        in_specs=[small, small, small, small, small, large, large],
        out_specs=(small, small),
        scratch_shapes=[
            pltpu.VMEM((8, owned), f32),
            pltpu.VMEM((channels, rows), b16),
            pltpu.VMEM((steps, 128), f32),
            pltpu.VMEM((steps, rows), b16),
            pltpu.VMEM((NSUB, 4, 2, rows, width), b16),
            pltpu.VMEM((modes, points), b16),
            pltpu.VMEM((4, NSUB, steps, width), b16),
            pltpu.VMEM((4, NSUB, steps, width), b16),
            pltpu.VMEM((NSUB, 4, steps, width), f32),
        ] + [pltpu.VMEM((NSUB, steps, width), b16)] * 6 + [
            pltpu.VMEM((NSUB, width // 128, steps, 128), f32),
            pltpu.VMEM((NSUB, 8, width), f32),
            pltpu.VMEM((tms - 1, NSUB, 8, width), f32),
            pltpu.VMEM((NSUB, 8, width), f32),
            pltpu.VMEM((steps, modes), b16),
            pltpu.VMEM((steps, points), f32),
            pltpu.SemaphoreType.DMA((NSUB, kinds)),
            pltpu.SemaphoreType.DMA((NSUB, kinds)),
            pltpu.SemaphoreType.DMA((NSUB, 4, 2)),
            pltpu.SemaphoreType.DMA((NSUB, 4, 2)),
        ],
        compiler_params=pltpu.CompilerParams(
            collective_id=0, has_side_effects=True, vmem_limit_bytes=50 * 1024 * 1024
        ),
        cost_estimate=pl.CostEstimate(
            flops=2 * steps * (modes * (points + rows) + channels * rows),
            bytes_accessed=2 * (modes * points + rows * modes + steps * points),
            transcendentals=0,
        ),
    )(damping.reshape(1, owned), frequency.reshape(1, owned), gains, load_index.reshape(1, channels), loads, phi, shapes)
    return hand_over(*results)


def carried_in(value, axis, join, neutral):
    count, mine = (lax.axis_size(axis), lax.axis_index(axis))
    pieces = jax.tree.map(lambda part: lax.all_gather(part, axis), value)
    subtotal = jax.tree.map(
        lambda part, zero: jnp.full_like(part, 0) + jnp.asarray(zero, part.dtype), value, neutral
    )

    def step(position, subtotal):
        longer = join(subtotal, jax.tree.map(lambda part: part[position], pieces))
        return jax.tree.map(lambda new, old: jnp.where(position < mine, new, old), longer, subtotal)

    return lax.fori_loop(0, count - 1, step, subtotal)


def combine(earlier, later):
    ear, eai, ebr, ebi = earlier
    lar, lai, lbr, lbi = later
    return (
        lar * ear - lai * eai,
        lar * eai + lai * ear,
        lar * ebr - lai * ebi + lbr,
        lar * ebi + lai * ebr + lbi,
    )


def body(loads, phi, load_index, damping, frequency, gains, shapes):
    owned = damping.shape[0]
    steps = loads.shape[0]
    rows_here = phi.shape[0]
    local_index = load_index - lax.axis_index("dof") * rows_here
    selected = jnp.take(phi, local_index, axis=0)
    columns = lax.all_to_all(selected, "dof", split_axis=1, concat_axis=0, tiled=True)
    block = columns
    modal = lax.dot_general(
        block,
        lax.all_gather(loads, "dof", axis=1, tiled=True),
        (((0,), (1,)), ((), ())),
        preferred_element_type=jnp.float32,
    )
    drive = jnp.sqrt(-jnp.expm1(-2.0 * damping))
    width = min(128, steps)
    blocks = steps // width
    log_gain = jnp.cumsum(jnp.log(gains).reshape(blocks, width), axis=1)
    rise = jnp.exp(log_gain)
    fall = jnp.exp(-log_gain)
    offsets = jnp.arange(width, dtype=jnp.float32)
    lag = offsets[:, None] - offsets[None, :]
    lower = lag >= 0.0
    lag_pos = jnp.where(lower, lag, 0.0)
    decay = jnp.exp(-damping[:, None, None] * lag_pos[None, :, :])
    turn = frequency[:, None, None] * lag_pos[None, :, :]
    kernel_re = jnp.where(lower[None, :, :], decay * jnp.cos(turn), 0.0)
    kernel_im = jnp.where(lower[None, :, :], decay * jnp.sin(turn), 0.0)
    pushed = (drive[:, None] * modal).reshape(owned, blocks, width) * fall[None, :, :]
    local_re = (
        jnp.einsum("mts,mns->mnt", kernel_re, pushed, precision=lax.Precision.HIGHEST)
        * rise[None, :, :]
    )
    local_im = (
        jnp.einsum("mts,mns->mnt", kernel_im, pushed, precision=lax.Precision.HIGHEST)
        * rise[None, :, :]
    )
    ahead = offsets + 1.0
    power_mag = jnp.exp(-damping[:, None] * ahead[None, :])
    power_re = power_mag * jnp.cos(frequency[:, None] * ahead[None, :])
    power_im = power_mag * jnp.sin(frequency[:, None] * ahead[None, :])
    carry_re_all = power_re[:, None, :] * rise[None, :, :]
    carry_im_all = power_im[:, None, :] * rise[None, :, :]
    unit = jnp.ones((owned,), jnp.float32)
    nothing = jnp.zeros((owned,), jnp.float32)
    running = (unit, nothing, nothing, nothing)
    entering = []
    for index in range(blocks):
        entering.append(running)
        piece = (
            carry_re_all[:, index, width - 1],
            carry_im_all[:, index, width - 1],
            local_re[:, index, width - 1],
            local_im[:, index, width - 1],
        )
        running = combine(running, piece)
    incoming = carried_in(running, "tm", combine, (unit, nothing, nothing, nothing))
    state_re = []
    state_im = []
    for index in range(blocks):
        joined = combine(incoming, entering[index])
        state_re.append(joined[2])
        state_im.append(joined[3])
    enter_re = jnp.stack(state_re, axis=1)
    enter_im = jnp.stack(state_im, axis=1)
    history = (
        carry_re_all * enter_re[:, :, None] - carry_im_all * enter_im[:, :, None] + local_re
    ).reshape(owned, steps)
    rounded = history.astype(jnp.bfloat16)
    block = shapes
    field = lax.dot_general(
        lax.all_gather(rounded, "dof", axis=0, tiled=True),
        block,
        (((0,), (0,)), ((), ())),
        preferred_element_type=jnp.float32,
    )
    return (field.astype(jnp.bfloat16), history)


def solution(mesh):
    placed = (P("tm", "dof"), P("dof", None), P("dof"), P("dof"), P("dof"), P("tm"), P(None, "dof"))
    part = functools.partial(fused, mesh.shape["tm"]) if mesh.shape["dof"] == 8 else body
    return jax.shard_map(
        part,
        mesh=mesh,
        in_specs=placed,
        out_specs=(P("tm", "dof"), P("dof", "tm")),
        check_vma=False,
    )
```

```python
import functools

import jax
import jax.numpy as jnp
from jax import lax
from jax.experimental import pallas as pl
from jax.experimental.pallas import tpu as pltpu
from jax.sharding import PartitionSpec as P

MESH = pl.DeviceIdType.MESH
NSUB = 2
BLOCKS = ((0, 0), (0, 1), (1, 0), (2, 0), (1, 1), (2, 1), (3, 0), (3, 1))
SEGS = 16
CORE, DA, DB, XA, XB, YA, YB = 0, 4, 5, 6, 7, 8, 9
GXA, GXB, GYA, GYB, GP, FA, FB, PX, PY, PD, TM = 10, 11, 12, 13, 14, 15, 16, 17, 18, 19, 20


def cmul(ar, ai, br, bi):
    return ar * br - ai * bi, ar * bi + ai * br


def power(ar, ai, exponent):
    result = None
    while exponent:
        if exponent & 1:
            result = (ar, ai) if result is None else cmul(*result, ar, ai)
        exponent >>= 1
        if exponent:
            ar, ai = cmul(ar, ai, ar, ai)
    return result


def kernel(
    tms, packed, loads, phi, shapes, field, hist,
    pars, onehot, spread, row_loads, phi_buf, shapes_buf, tx_core, rx_core, own, tx_d, tx_x, tx_y, rx_d, rx_x, rx_y,
    mod, tx_tm, rx_tm, carry, gath, acc,
    send, recv, phi_sem, shapes_sem,
):
    steps = loads.shape[0]
    half = steps // 2
    owned = pars.shape[1]
    damping = packed[pl.ds(0, owned)].reshape(1, owned)
    frequency = packed[pl.ds(owned, owned)].reshape(1, owned)
    index = packed[pl.ds(2 * owned, loads.shape[1])].reshape(1, loads.shape[1])
    gains = packed[pl.ds(2 * owned + loads.shape[1], steps)].reshape(1, steps)
    width = owned // NSUB
    cols = width // 128
    seg = steps // SEGS
    rows = phi.shape[0]
    channels = loads.shape[1]
    points = shapes.shape[1]
    tile = min(512, points)
    top, low = pl.ds(0, half), pl.ds(half, half)

    d = lax.axis_index("dof")
    me = lax.axis_index("tm")
    core = lax.rem(d, 2)
    px = lax.rem(d // 2, 2)
    py = d // 4
    other = 1 - core
    partner = d + 1 - 2 * core
    xn = d + 2 * (1 - 2 * px)
    yn = d + 4 * (1 - 2 * py)

    def owner(q, cc):
        fx, fy = q % 2, q // 2
        x = px + fx * (1 - 2 * px)
        y = py + fy * (1 - 2 * py)
        return (y * 2 + x) * 2 + cc

    def remote(src, dst, kind, s, to):
        return pltpu.make_async_remote_copy(
            src_ref=src, dst_ref=dst, send_sem=send.at[s, kind], recv_sem=recv.at[s, kind],
            device_id={"dof": to}, device_id_type=MESH,
        )

    def core_copy(q, s):
        return remote(tx_core.at[q, s], rx_core.at[q, s], CORE + q, s, partner)

    def piece(src, dst, span, kind, s, to):
        return remote(src.at[s, span], dst.at[s, span], kind, s, to)

    def da(s):
        return piece(tx_d, rx_d, top, DA, s, xn)

    def db(s):
        return piece(tx_d, rx_d, low, DB, s, yn)

    def xa(s):
        return piece(tx_x, rx_x, top, XA, s, xn)

    def xb(s):
        return piece(tx_x, rx_x, low, XB, s, xn)

    def ya(s):
        return piece(tx_y, rx_y, top, YA, s, yn)

    def yb(s):
        return piece(tx_y, rx_y, low, YB, s, yn)

    def lanes_of(q, r, s):
        return pl.ds((s * 8 + BLOCKS.index((q, r))) * width, width)

    def gathered(src, dst, span, kind, s, to):
        return remote(gath.at[span, lanes_of(*src, s)], gath.at[span, lanes_of(*dst, s)], kind, s, to)

    whole = pl.ds(0, steps)

    def gxa(s):
        return gathered((0, 0), (1, 0), top, GXA, s, xn)

    def gxb(s):
        return gathered((0, 0), (1, 0), low, GXB, s, xn)

    def gya(s):
        return gathered((0, 0), (2, 0), top, GYA, s, yn)

    def gyb(s):
        return gathered((0, 0), (2, 0), low, GYB, s, yn)

    def gp(s):
        return gathered((0, 0), (0, 1), whole, GP, s, partner)

    def fa(s):
        return gathered((1, 0), (3, 0), top, FA, s, yn)

    def fb(s):
        return gathered((2, 0), (3, 0), low, FB, s, xn)

    def pq(q, s):
        return gathered((q, 0), (q, 1), whole, PX + q - 1, s, partner)

    def state_copy(dk, s, to):
        return pltpu.make_async_remote_copy(
            src_ref=tx_tm.at[s], dst_ref=rx_tm.at[dk - 1, s],
            send_sem=send.at[s, TM + dk - 1], recv_sem=recv.at[s, TM + dk - 1],
            device_id={"tm": to}, device_id_type=MESH,
        )

    def phi_copy(q, r, s):
        start = pl.multiple_of(owner(q, other if r else core) * owned + s * width, width)
        return pltpu.make_async_copy(
            phi.at[:, pl.ds(start, width)], phi_buf.at[s, q, r], phi_sem.at[s, q, r]
        )

    def shapes_copy(q, r, s):
        start = pl.multiple_of(owner(q, other if r else core) * owned + s * width, width)
        return pltpu.make_async_copy(
            shapes.at[pl.ds(start, width), :], shapes_buf.at[lanes_of(q, r, s), :], shapes_sem.at[s, q, r]
        )

    order = (3, 1, 2, 0)

    barrier = pltpu.get_barrier_semaphore()
    for to in (partner, xn, yn):
        pl.semaphore_signal(barrier, inc=1, device_id={"dof": to}, device_id_type=MESH)
    for dk in range(1, tms):
        to = lax.rem(me + dk, tms)
        pl.semaphore_signal(barrier, inc=1, device_id={"tm": to}, device_id_type=MESH)
    def start_phi(s):
        for q in order:
            phi_copy(q, 1, s).start()
            phi_copy(q, 0, s).start()

    start_phi(0)

    names = jnp.broadcast_to(index - (d * rows).astype(jnp.float32), (128, channels)).T
    for j in range(rows // 128):
        place = (lax.broadcasted_iota(jnp.int32, (channels, 128), 1) + j * 128).astype(jnp.float32)
        onehot[:, j * 128:(j + 1) * 128] = jnp.where(place == names, 1.0, 0.0).astype(jnp.bfloat16)
    row_loads[...] = jnp.dot(loads[...], onehot[...], preferred_element_type=jnp.float32).astype(jnp.bfloat16)

    def partial_modal(q, r, s):
        phi_copy(q, r, s).wait()
        return jnp.dot(row_loads[...], phi_buf[s, q, r], preferred_element_type=jnp.float32)

    def for_partner(q, s):
        tx_core[q, s] = partial_modal(q, 1, s).astype(jnp.bfloat16)
        if q == order[0] and s == 0:
            start_phi(1)
            pl.semaphore_wait(barrier, 3 + tms - 1)
        core_copy(q, s).start()

    def chip_sum(q, s, span):
        return own[s, q, span] + rx_core[q, s, span].astype(jnp.float32)

    def to_chip(q, s):
        core_copy(q, s).wait_recv()
        if q == 3:
            tx_d[s] = chip_sum(q, s, pl.ds(0, steps)).astype(jnp.bfloat16)
            da(s).start()
            db(s).start()
        if q == 1:
            tx_x[s, top] = chip_sum(q, s, top).astype(jnp.bfloat16)
            xa(s).start()
        if q == 2:
            tx_y[s, low] = chip_sum(q, s, low).astype(jnp.bfloat16)
            yb(s).start()

    def partials(s, between=None):
        for n, q in enumerate(order):
            for_partner(q, s)
            if n:
                to_chip(order[n - 1], s)
            if between is not None and n == 2:
                between()
            own[s, q] = partial_modal(q, 0, s)

    def parameters():
        x = 2.0 * damping
        series = jnp.ones_like(x)
        for n in range(12, 1, -1):
            series = 1.0 - x * series / n
        drive = jnp.sqrt(jnp.where(x < 0.5, x * series, 1.0 - jnp.exp(-x)))
        radius = jnp.exp(-damping)
        pars[0:1, :] = radius * jnp.cos(frequency)
        pars[1:2, :] = radius * jnp.sin(frequency)
        pars[2:3, :] = drive
        spread[...] = jnp.broadcast_to(gains, (128, steps)).T

    def pass_on(s):
        db(s).wait_recv()
        tx_x[s, low] = (chip_sum(1, s, low) + rx_d[s, low].astype(jnp.float32)).astype(jnp.bfloat16)
        xb(s).start()
        da(s).wait_recv()
        tx_y[s, top] = (chip_sum(2, s, top) + rx_d[s, top].astype(jnp.float32)).astype(jnp.bfloat16)
        ya(s).start()

    def par(s, j):
        lanes = slice(s * width + j * 128, s * width + (j + 1) * 128)
        return pars[0:1, lanes], pars[1:2, lanes], pars[2:3, lanes]

    def scan(s, start, store):
        coefs = [tuple(jnp.broadcast_to(v, (SEGS, 128)) for v in par(s, j)[:2]) for j in range(cols)]

        def step(i, state):
            total, waves = state
            at = pl.ds(i, SEGS, stride=seg)
            gain = spread[at, :]
            out = []
            for j in range(cols):
                cr, ci = gain * coefs[j][0], gain * coefs[j][1]
                wr, wi = waves[j]
                re = (cr * wr + mod[s, j, at, :]) - ci * wi
                im = cr * wi + ci * wr
                if store:
                    mod[s, j, at, :] = re
                out.append((re, im))
            return total * gain, tuple(out)

        one = jnp.ones((SEGS, 128), jnp.float32)
        return lax.fori_loop(0, seg, step, (one, tuple(start)), unroll=8)

    def local_states(s):
        for copy in (core_copy(0, s), xa(s), xb(s), ya(s), yb(s)):
            copy.wait_recv()
        for j in range(cols):
            lanes = slice(j * 128, (j + 1) * 128)
            value = own[s, 0, :, lanes]
            for part in (rx_core.at[0], rx_x, rx_y):
                value += part[s, :, lanes].astype(jnp.float32)
            mod[s, j] = value * par(s, j)[2]
        zero = jnp.zeros((SEGS, 128), jnp.float32)
        total, ends = scan(s, [(zero, zero)] * cols, False)
        kept = []
        for j in range(cols):
            lanes = slice(j * 128, (j + 1) * 128)
            a, b, _ = par(s, j)
            ar, ai = power(a, b, seg)
            state = (jnp.zeros((1, 128), jnp.float32),) * 2
            prod = (jnp.ones((1, 128), jnp.float32), jnp.zeros((1, 128), jnp.float32))
            entering, products = [], []
            gain = jnp.ones((1, 128), jnp.float32)
            for k in range(SEGS):
                entering.append(state)
                products.append(prod)
                g = total[k:k + 1]
                c = (ar * g, ai * g)
                moved = cmul(*c, *state)
                state = (moved[0] + ends[j][0][k:k + 1], moved[1] + ends[j][1][k:k + 1])
                prod = cmul(*c, *prod)
                gain = gain * g
            tx_tm[s, 0:1, lanes] = state[0]
            tx_tm[s, 1:2, lanes] = state[1]
            tx_tm[s, 2:3, lanes] = gain
            kept.append(tuple(
                jnp.concatenate([v[n] for v in some], axis=0) for some in (entering, products) for n in (0, 1)
            ))
        for dk in range(1, tms):
            @pl.when(me + dk < tms)
            def _():
                state_copy(dk, s, me + dk).start()
        return kept

    def finish(s, kept):
        carry[s] = jnp.zeros(carry.shape[1:], jnp.float32)
        for dk in range(tms - 1, 0, -1):
            @pl.when(me >= dk)
            def _():
                state_copy(dk, s, me).wait_recv()
                for j in range(cols):
                    lanes = slice(j * 128, (j + 1) * 128)
                    a, b, _ = par(s, j)
                    ar, ai = power(a, b, steps)
                    gain = rx_tm[dk - 1, s, 2:3, lanes]
                    re, im = cmul(ar * gain, ai * gain, carry[s, 0:1, lanes], carry[s, 1:2, lanes])
                    carry[s, 0:1, lanes] = re + rx_tm[dk - 1, s, 0:1, lanes]
                    carry[s, 1:2, lanes] = im + rx_tm[dk - 1, s, 1:2, lanes]
        start = []
        for j in range(cols):
            lanes = slice(j * 128, (j + 1) * 128)
            er, ei, kr, ki = kept[j]
            re, im = cmul(kr, ki, carry[s, 0:1, lanes], carry[s, 1:2, lanes])
            start.append((er + re, ei + im))
        scan(s, start, True)
        for j in range(cols):
            gath[:, pl.ds(s * 8 * width + j * 128, 128)] = mod[s, j].astype(jnp.bfloat16)
        for copy in (gxa(s), gyb(s), gp(s), gxb(s), gya(s)):
            copy.start()
        for j in range(cols):
            hist[s * width + j * 128:s * width + (j + 1) * 128, :] = mod[s, j].T

    def forward(s):
        gxa(s).wait_recv()
        fa(s).start()
        gyb(s).wait_recv()
        fb(s).start()

    def share(s):
        gxb(s).wait_recv()
        pq(1, s).start()
        gya(s).wait_recv()
        pq(2, s).start()

    def share_last(s):
        fa(s).wait_recv()
        fb(s).wait_recv()
        pq(3, s).start()

    def expand(first, count, mode):
        for block in range(first, first + count):
            shapes_copy(*BLOCKS[block % 8], block // 8).wait()
        deep = pl.ds(first * width, count * width)

        def one(n, _):
            at = pl.ds(pl.multiple_of(n * tile, tile), tile)
            value = jnp.dot(gath[:, deep], shapes_buf[deep, at], preferred_element_type=jnp.float32)
            if mode != "first":
                value += acc[:, at]
            if mode == "last":
                field[:, at] = value.astype(jnp.bfloat16)
            else:
                acc[:, at] = value
            return 0

        lax.fori_loop(0, points // tile, one, 0)

    partials(0)
    for s in range(NSUB):
        for q, r in BLOCKS:
            shapes_copy(q, r, s).start()
    parameters()
    partials(1, lambda: pass_on(0))
    kept_0 = local_states(0)
    pass_on(1)
    finish(0, kept_0)
    kept_1 = local_states(1)
    gp(0).wait_recv()
    expand(0, 2, "first")
    forward(0)
    finish(1, kept_1)
    share(0)
    expand(2, 2, "add")
    share_last(0)
    pq(1, 0).wait_recv()
    pq(2, 0).wait_recv()
    expand(4, 2, "add")
    forward(1)
    pq(3, 0).wait_recv()
    gp(1).wait_recv()
    expand(6, 4, "add")
    share(1)
    expand(10, 2, "add")
    pq(1, 1).wait_recv()
    pq(2, 1).wait_recv()
    expand(12, 2, "add")
    share_last(1)
    expand(14, 1, "add")
    pq(3, 1).wait_recv()
    expand(15, 1, "last")

    for s in range(NSUB):
        for q in range(4):
            core_copy(q, s).wait_send()
        for copy in (
            da(s), db(s), xa(s), xb(s), ya(s), yb(s), gxa(s), gxb(s), gya(s), gyb(s), gp(s), fa(s), fb(s),
            pq(1, s), pq(2, s), pq(3, s),
        ):
            copy.wait_send()
        for dk in range(1, tms):
            @pl.when(me + dk < tms)
            def _():
                state_copy(dk, s, me).wait_send()


def hand_over(*arrays):
    pieces = 4

    def copies(*refs):
        count = len(arrays)
        started = []
        for n in range(count):
            rows = arrays[n].shape[0] // pieces
            for piece in range(pieces):
                at = pl.ds(piece * rows, rows)
                started.append(
                    pltpu.make_async_copy(refs[n].at[at], refs[count + n].at[at], refs[2 * count].at[n, piece])
                )
        for copy in started:
            copy.start()
        for copy in started:
            copy.wait()

    return pl.pallas_call(
        copies,
        out_shape=tuple(jax.ShapeDtypeStruct(a.shape, a.dtype) for a in arrays),
        in_specs=[pl.BlockSpec(memory_space=pltpu.VMEM)] * len(arrays),
        out_specs=(pl.BlockSpec(memory_space=pltpu.HBM),) * len(arrays),
        scratch_shapes=[pltpu.SemaphoreType.DMA((len(arrays), pieces))],
        compiler_params=pltpu.CompilerParams(vmem_limit_bytes=16 * 1024 * 1024),
        cost_estimate=pl.CostEstimate(
            flops=0, bytes_accessed=sum(2 * a.size * a.dtype.itemsize for a in arrays), transcendentals=0
        ),
    )(*arrays)


def fused(tms, loads, phi, load_index, damping, frequency, gains, shapes):
    owned, steps, channels = damping.shape[0], loads.shape[0], loads.shape[1]
    rows, points, modes = phi.shape[0], shapes.shape[1], shapes.shape[0]
    width = owned // NSUB
    b16, f32 = jnp.bfloat16, jnp.float32
    packed = jnp.concatenate([damping, frequency, load_index.astype(f32), gains])
    kinds = TM + tms - 1
    small = pl.BlockSpec(memory_space=pltpu.VMEM)
    large = pl.BlockSpec(memory_space=pltpu.HBM)
    results = pl.pallas_call(
        functools.partial(kernel, tms),
        out_shape=(
            jax.ShapeDtypeStruct((steps, points), b16),
            jax.ShapeDtypeStruct((owned, steps), f32),
        ),
        in_specs=[small, small, large, large],
        out_specs=(small, small),
        scratch_shapes=[
            pltpu.VMEM((8, owned), f32),
            pltpu.VMEM((channels, rows), b16),
            pltpu.VMEM((steps, 128), f32),
            pltpu.VMEM((steps, rows), b16),
            pltpu.VMEM((NSUB, 4, 2, rows, width), b16),
            pltpu.VMEM((modes, points), b16),
            pltpu.VMEM((4, NSUB, steps, width), b16),
            pltpu.VMEM((4, NSUB, steps, width), b16),
            pltpu.VMEM((NSUB, 4, steps, width), f32),
        ] + [pltpu.VMEM((NSUB, steps, width), b16)] * 6 + [
            pltpu.VMEM((NSUB, width // 128, steps, 128), f32),
            pltpu.VMEM((NSUB, 8, width), f32),
            pltpu.VMEM((tms - 1, NSUB, 8, width), f32),
            pltpu.VMEM((NSUB, 8, width), f32),
            pltpu.VMEM((steps, modes), b16),
            pltpu.VMEM((steps, points), f32),
            pltpu.SemaphoreType.DMA((NSUB, kinds)),
            pltpu.SemaphoreType.DMA((NSUB, kinds)),
            pltpu.SemaphoreType.DMA((NSUB, 4, 2)),
            pltpu.SemaphoreType.DMA((NSUB, 4, 2)),
        ],
        compiler_params=pltpu.CompilerParams(
            collective_id=0, has_side_effects=True, vmem_limit_bytes=50 * 1024 * 1024
        ),
        cost_estimate=pl.CostEstimate(
            flops=2 * steps * (modes * (points + rows) + channels * rows),
            bytes_accessed=2 * (modes * points + rows * modes + steps * points),
            transcendentals=0,
        ),
    )(packed, loads, phi, shapes)
    return hand_over(*results)


def carried_in(value, axis, join, neutral):
    count, mine = (lax.axis_size(axis), lax.axis_index(axis))
    pieces = jax.tree.map(lambda part: lax.all_gather(part, axis), value)
    subtotal = jax.tree.map(
        lambda part, zero: jnp.full_like(part, 0) + jnp.asarray(zero, part.dtype), value, neutral
    )

    def step(position, subtotal):
        longer = join(subtotal, jax.tree.map(lambda part: part[position], pieces))
        return jax.tree.map(lambda new, old: jnp.where(position < mine, new, old), longer, subtotal)

    return lax.fori_loop(0, count - 1, step, subtotal)


def combine(earlier, later):
    ear, eai, ebr, ebi = earlier
    lar, lai, lbr, lbi = later
    return (
        lar * ear - lai * eai,
        lar * eai + lai * ear,
        lar * ebr - lai * ebi + lbr,
        lar * ebi + lai * ebr + lbi,
    )


def body(loads, phi, load_index, damping, frequency, gains, shapes):
    owned = damping.shape[0]
    steps = loads.shape[0]
    rows_here = phi.shape[0]
    local_index = load_index - lax.axis_index("dof") * rows_here
    selected = jnp.take(phi, local_index, axis=0)
    columns = lax.all_to_all(selected, "dof", split_axis=1, concat_axis=0, tiled=True)
    block = columns
    modal = lax.dot_general(
        block,
        lax.all_gather(loads, "dof", axis=1, tiled=True),
        (((0,), (1,)), ((), ())),
        preferred_element_type=jnp.float32,
    )
    drive = jnp.sqrt(-jnp.expm1(-2.0 * damping))
    width = min(128, steps)
    blocks = steps // width
    log_gain = jnp.cumsum(jnp.log(gains).reshape(blocks, width), axis=1)
    rise = jnp.exp(log_gain)
    fall = jnp.exp(-log_gain)
    offsets = jnp.arange(width, dtype=jnp.float32)
    lag = offsets[:, None] - offsets[None, :]
    lower = lag >= 0.0
    lag_pos = jnp.where(lower, lag, 0.0)
    decay = jnp.exp(-damping[:, None, None] * lag_pos[None, :, :])
    turn = frequency[:, None, None] * lag_pos[None, :, :]
    kernel_re = jnp.where(lower[None, :, :], decay * jnp.cos(turn), 0.0)
    kernel_im = jnp.where(lower[None, :, :], decay * jnp.sin(turn), 0.0)
    pushed = (drive[:, None] * modal).reshape(owned, blocks, width) * fall[None, :, :]
    local_re = (
        jnp.einsum("mts,mns->mnt", kernel_re, pushed, precision=lax.Precision.HIGHEST)
        * rise[None, :, :]
    )
    local_im = (
        jnp.einsum("mts,mns->mnt", kernel_im, pushed, precision=lax.Precision.HIGHEST)
        * rise[None, :, :]
    )
    ahead = offsets + 1.0
    power_mag = jnp.exp(-damping[:, None] * ahead[None, :])
    power_re = power_mag * jnp.cos(frequency[:, None] * ahead[None, :])
    power_im = power_mag * jnp.sin(frequency[:, None] * ahead[None, :])
    carry_re_all = power_re[:, None, :] * rise[None, :, :]
    carry_im_all = power_im[:, None, :] * rise[None, :, :]
    unit = jnp.ones((owned,), jnp.float32)
    nothing = jnp.zeros((owned,), jnp.float32)
    running = (unit, nothing, nothing, nothing)
    entering = []
    for index in range(blocks):
        entering.append(running)
        piece = (
            carry_re_all[:, index, width - 1],
            carry_im_all[:, index, width - 1],
            local_re[:, index, width - 1],
            local_im[:, index, width - 1],
        )
        running = combine(running, piece)
    incoming = carried_in(running, "tm", combine, (unit, nothing, nothing, nothing))
    state_re = []
    state_im = []
    for index in range(blocks):
        joined = combine(incoming, entering[index])
        state_re.append(joined[2])
        state_im.append(joined[3])
    enter_re = jnp.stack(state_re, axis=1)
    enter_im = jnp.stack(state_im, axis=1)
    history = (
        carry_re_all * enter_re[:, :, None] - carry_im_all * enter_im[:, :, None] + local_re
    ).reshape(owned, steps)
    rounded = history.astype(jnp.bfloat16)
    block = shapes
    field = lax.dot_general(
        lax.all_gather(rounded, "dof", axis=0, tiled=True),
        block,
        (((0,), (0,)), ((), ())),
        preferred_element_type=jnp.float32,
    )
    return (field.astype(jnp.bfloat16), history)


def solution(mesh):
    placed = (P("tm", "dof"), P("dof", None), P("dof"), P("dof"), P("dof"), P("tm"), P(None, "dof"))
    part = functools.partial(fused, mesh.shape["tm"]) if mesh.shape["dof"] == 8 else body
    return jax.shard_map(
        part,
        mesh=mesh,
        in_specs=placed,
        out_specs=(P("tm", "dof"), P("dof", "tm")),
        check_vma=False,
    )
```

```python
import functools

import jax
import jax.numpy as jnp
from jax import lax
from jax.experimental import pallas as pl
from jax.experimental.pallas import tpu as pltpu
from jax.sharding import PartitionSpec as P

MESH = pl.DeviceIdType.MESH
NSUB = 4
BLOCKS = ((0, 0), (0, 1), (1, 0), (2, 0), (1, 1), (2, 1), (3, 0), (3, 1))
SEGS = 16
CORE, DA, DB, XA, XB, YA, YB = 0, 4, 5, 6, 7, 8, 9
GXA, GXB, GYA, GYB, GP, FA, FB, PX, PY, PD, TM = 10, 11, 12, 13, 14, 15, 16, 17, 18, 19, 20


def cmul(ar, ai, br, bi):
    return ar * br - ai * bi, ar * bi + ai * br


def power(ar, ai, exponent):
    result = None
    while exponent:
        if exponent & 1:
            result = (ar, ai) if result is None else cmul(*result, ar, ai)
        exponent >>= 1
        if exponent:
            ar, ai = cmul(ar, ai, ar, ai)
    return result


def kernel(
    tms, packed, loads, phi, shapes, field, hist,
    pars, onehot, spread, row_loads, phi_buf, shapes_buf, tx_core, rx_core, own, tx_d, tx_x, tx_y, rx_d, rx_x, rx_y,
    mod, tx_tm, rx_tm, carry, gath, acc,
    send, recv, phi_sem, shapes_sem,
):
    steps = loads.shape[0]
    half = steps // 2
    owned = pars.shape[1]
    damping = packed[pl.ds(0, owned)].reshape(1, owned)
    frequency = packed[pl.ds(owned, owned)].reshape(1, owned)
    index = packed[pl.ds(2 * owned, loads.shape[1])].reshape(1, loads.shape[1])
    gains = packed[pl.ds(2 * owned + loads.shape[1], steps)].reshape(1, steps)
    width = owned // NSUB
    cols = width // 128
    seg = steps // SEGS
    rows = phi.shape[0]
    channels = loads.shape[1]
    points = shapes.shape[1]
    tile = min(512, points)
    top, low = pl.ds(0, half), pl.ds(half, half)

    d = lax.axis_index("dof")
    me = lax.axis_index("tm")
    core = lax.rem(d, 2)
    px = lax.rem(d // 2, 2)
    py = d // 4
    other = 1 - core
    partner = d + 1 - 2 * core
    xn = d + 2 * (1 - 2 * px)
    yn = d + 4 * (1 - 2 * py)

    def owner(q, cc):
        fx, fy = q % 2, q // 2
        x = px + fx * (1 - 2 * px)
        y = py + fy * (1 - 2 * py)
        return (y * 2 + x) * 2 + cc

    def remote(src, dst, kind, s, to):
        return pltpu.make_async_remote_copy(
            src_ref=src, dst_ref=dst, send_sem=send.at[s, kind], recv_sem=recv.at[s, kind],
            device_id={"dof": to}, device_id_type=MESH,
        )

    def core_copy(q, s):
        return remote(tx_core.at[q, s], rx_core.at[q, s], CORE + q, s, partner)

    def piece(src, dst, span, kind, s, to):
        return remote(src.at[s, span], dst.at[s, span], kind, s, to)

    def da(s):
        return piece(tx_d, rx_d, top, DA, s, xn)

    def db(s):
        return piece(tx_d, rx_d, low, DB, s, yn)

    def xa(s):
        return piece(tx_x, rx_x, top, XA, s, xn)

    def xb(s):
        return piece(tx_x, rx_x, low, XB, s, xn)

    def ya(s):
        return piece(tx_y, rx_y, top, YA, s, yn)

    def yb(s):
        return piece(tx_y, rx_y, low, YB, s, yn)

    def lanes_of(q, r, s):
        return pl.ds((s * 8 + BLOCKS.index((q, r))) * width, width)

    def gathered(src, dst, span, kind, s, to):
        return remote(gath.at[span, lanes_of(*src, s)], gath.at[span, lanes_of(*dst, s)], kind, s, to)

    whole = pl.ds(0, steps)

    def gxa(s):
        return gathered((0, 0), (1, 0), top, GXA, s, xn)

    def gxb(s):
        return gathered((0, 0), (1, 0), low, GXB, s, xn)

    def gya(s):
        return gathered((0, 0), (2, 0), top, GYA, s, yn)

    def gyb(s):
        return gathered((0, 0), (2, 0), low, GYB, s, yn)

    def gp(s):
        return gathered((0, 0), (0, 1), whole, GP, s, partner)

    def fa(s):
        return gathered((1, 0), (3, 0), top, FA, s, yn)

    def fb(s):
        return gathered((2, 0), (3, 0), low, FB, s, xn)

    def pq(q, s):
        return gathered((q, 0), (q, 1), whole, PX + q - 1, s, partner)

    def state_copy(dk, s, to):
        return pltpu.make_async_remote_copy(
            src_ref=tx_tm.at[s], dst_ref=rx_tm.at[dk - 1, s],
            send_sem=send.at[s, TM + dk - 1], recv_sem=recv.at[s, TM + dk - 1],
            device_id={"tm": to}, device_id_type=MESH,
        )

    def phi_copy(q, r, s):
        start = pl.multiple_of(owner(q, other if r else core) * owned + s * width, width)
        return pltpu.make_async_copy(
            phi.at[:, pl.ds(start, width)], phi_buf.at[s, q, r], phi_sem.at[s, q, r]
        )

    def shapes_copy(q, r, s):
        start = pl.multiple_of(owner(q, other if r else core) * owned + s * width, width)
        return pltpu.make_async_copy(
            shapes.at[pl.ds(start, width), :], shapes_buf.at[lanes_of(q, r, s), :], shapes_sem.at[s, q, r]
        )

    order = (3, 1, 2, 0)

    barrier = pltpu.get_barrier_semaphore()
    for to in (partner, xn, yn):
        pl.semaphore_signal(barrier, inc=1, device_id={"dof": to}, device_id_type=MESH)
    for dk in range(1, tms):
        to = lax.rem(me + dk, tms)
        pl.semaphore_signal(barrier, inc=1, device_id={"tm": to}, device_id_type=MESH)
    def start_phi(s):
        for q in order:
            phi_copy(q, 1, s).start()
            phi_copy(q, 0, s).start()

    start_phi(0)

    names = jnp.broadcast_to(index - (d * rows).astype(jnp.float32), (128, channels)).T
    for j in range(rows // 128):
        place = (lax.broadcasted_iota(jnp.int32, (channels, 128), 1) + j * 128).astype(jnp.float32)
        onehot[:, j * 128:(j + 1) * 128] = jnp.where(place == names, 1.0, 0.0).astype(jnp.bfloat16)
    row_loads[...] = jnp.dot(loads[...], onehot[...], preferred_element_type=jnp.float32).astype(jnp.bfloat16)

    def partial_modal(q, r, s):
        phi_copy(q, r, s).wait()
        return jnp.dot(row_loads[...], phi_buf[s, q, r], preferred_element_type=jnp.float32)

    def for_partner(q, s):
        tx_core[q, s] = partial_modal(q, 1, s).astype(jnp.bfloat16)
        if q == order[0] and s == 0:
            for part in range(1, NSUB):
                start_phi(part)
            pl.semaphore_wait(barrier, 3 + tms - 1)
        core_copy(q, s).start()

    def chip_sum(q, s, span):
        return own[s, q, span] + rx_core[q, s, span].astype(jnp.float32)

    def to_chip(q, s):
        core_copy(q, s).wait_recv()
        if q == 3:
            tx_d[s] = chip_sum(q, s, pl.ds(0, steps)).astype(jnp.bfloat16)
            da(s).start()
            db(s).start()
        if q == 1:
            tx_x[s, top] = chip_sum(q, s, top).astype(jnp.bfloat16)
            xa(s).start()
        if q == 2:
            tx_y[s, low] = chip_sum(q, s, low).astype(jnp.bfloat16)
            yb(s).start()

    def partials(s, between=None):
        for n, q in enumerate(order):
            for_partner(q, s)
            if n:
                to_chip(order[n - 1], s)
            if between is not None and n == 2:
                between()
            own[s, q] = partial_modal(q, 0, s)

    def parameters():
        x = 2.0 * damping
        series = jnp.ones_like(x)
        for n in range(12, 1, -1):
            series = 1.0 - x * series / n
        drive = jnp.sqrt(jnp.where(x < 0.5, x * series, 1.0 - jnp.exp(-x)))
        radius = jnp.exp(-damping)
        pars[0:1, :] = radius * jnp.cos(frequency)
        pars[1:2, :] = radius * jnp.sin(frequency)
        pars[2:3, :] = drive
        spread[...] = jnp.broadcast_to(gains, (128, steps)).T

    def pass_on(s):
        db(s).wait_recv()
        tx_x[s, low] = (chip_sum(1, s, low) + rx_d[s, low].astype(jnp.float32)).astype(jnp.bfloat16)
        xb(s).start()
        da(s).wait_recv()
        tx_y[s, top] = (chip_sum(2, s, top) + rx_d[s, top].astype(jnp.float32)).astype(jnp.bfloat16)
        ya(s).start()

    def par(s, j):
        lanes = slice(s * width + j * 128, s * width + (j + 1) * 128)
        return pars[0:1, lanes], pars[1:2, lanes], pars[2:3, lanes]

    def scan(s, start, store):
        coefs = [tuple(jnp.broadcast_to(v, (SEGS, 128)) for v in par(s, j)[:2]) for j in range(cols)]

        def step(i, state):
            total, waves = state
            at = pl.ds(i, SEGS, stride=seg)
            gain = spread[at, :]
            out = []
            for j in range(cols):
                cr, ci = gain * coefs[j][0], gain * coefs[j][1]
                wr, wi = waves[j]
                re = (cr * wr + mod[s, j, at, :]) - ci * wi
                im = cr * wi + ci * wr
                if store:
                    mod[s, j, at, :] = re
                out.append((re, im))
            return total * gain, tuple(out)

        one = jnp.ones((SEGS, 128), jnp.float32)
        return lax.fori_loop(0, seg, step, (one, tuple(start)), unroll=8)

    def local_states(s):
        for copy in (core_copy(0, s), xa(s), xb(s), ya(s), yb(s)):
            copy.wait_recv()
        for j in range(cols):
            lanes = slice(j * 128, (j + 1) * 128)
            value = own[s, 0, :, lanes]
            for part in (rx_core.at[0], rx_x, rx_y):
                value += part[s, :, lanes].astype(jnp.float32)
            mod[s, j] = value * par(s, j)[2]
        zero = jnp.zeros((SEGS, 128), jnp.float32)
        total, ends = scan(s, [(zero, zero)] * cols, False)
        kept = []
        for j in range(cols):
            lanes = slice(j * 128, (j + 1) * 128)
            a, b, _ = par(s, j)
            ar, ai = power(a, b, seg)
            state = (jnp.zeros((1, 128), jnp.float32),) * 2
            prod = (jnp.ones((1, 128), jnp.float32), jnp.zeros((1, 128), jnp.float32))
            entering, products = [], []
            gain = jnp.ones((1, 128), jnp.float32)
            for k in range(SEGS):
                entering.append(state)
                products.append(prod)
                g = total[k:k + 1]
                c = (ar * g, ai * g)
                moved = cmul(*c, *state)
                state = (moved[0] + ends[j][0][k:k + 1], moved[1] + ends[j][1][k:k + 1])
                prod = cmul(*c, *prod)
                gain = gain * g
            tx_tm[s, 0:1, lanes] = state[0]
            tx_tm[s, 1:2, lanes] = state[1]
            tx_tm[s, 2:3, lanes] = gain
            kept.append(tuple(
                jnp.concatenate([v[n] for v in some], axis=0) for some in (entering, products) for n in (0, 1)
            ))
        for dk in range(1, tms):
            @pl.when(me + dk < tms)
            def _():
                state_copy(dk, s, me + dk).start()
        return kept

    def finish(s, kept):
        carry[s] = jnp.zeros(carry.shape[1:], jnp.float32)
        for dk in range(tms - 1, 0, -1):
            @pl.when(me >= dk)
            def _():
                state_copy(dk, s, me).wait_recv()
                for j in range(cols):
                    lanes = slice(j * 128, (j + 1) * 128)
                    a, b, _ = par(s, j)
                    ar, ai = power(a, b, steps)
                    gain = rx_tm[dk - 1, s, 2:3, lanes]
                    re, im = cmul(ar * gain, ai * gain, carry[s, 0:1, lanes], carry[s, 1:2, lanes])
                    carry[s, 0:1, lanes] = re + rx_tm[dk - 1, s, 0:1, lanes]
                    carry[s, 1:2, lanes] = im + rx_tm[dk - 1, s, 1:2, lanes]
        start = []
        for j in range(cols):
            lanes = slice(j * 128, (j + 1) * 128)
            er, ei, kr, ki = kept[j]
            re, im = cmul(kr, ki, carry[s, 0:1, lanes], carry[s, 1:2, lanes])
            start.append((er + re, ei + im))
        scan(s, start, True)
        for j in range(cols):
            gath[:, pl.ds(s * 8 * width + j * 128, 128)] = mod[s, j].astype(jnp.bfloat16)
        for copy in (gxa(s), gyb(s), gp(s), gxb(s), gya(s)):
            copy.start()
        for j in range(cols):
            hist[s * width + j * 128:s * width + (j + 1) * 128, :] = mod[s, j].T

    def forward(s):
        gxa(s).wait_recv()
        fa(s).start()
        gyb(s).wait_recv()
        fb(s).start()

    def share(s):
        gxb(s).wait_recv()
        pq(1, s).start()
        gya(s).wait_recv()
        pq(2, s).start()

    def share_last(s):
        fa(s).wait_recv()
        fb(s).wait_recv()
        pq(3, s).start()

    def expand(first, count, mode):
        for block in range(first, first + count):
            shapes_copy(*BLOCKS[block % 8], block // 8).wait()
        deep = pl.ds(first * width, count * width)

        def one(n, _):
            at = pl.ds(pl.multiple_of(n * tile, tile), tile)
            value = jnp.dot(gath[:, deep], shapes_buf[deep, at], preferred_element_type=jnp.float32)
            if mode != "first":
                value += acc[:, at]
            if mode == "last":
                field[:, at] = value.astype(jnp.bfloat16)
            else:
                acc[:, at] = value
            return 0

        lax.fori_loop(0, points // tile, one, 0)

    def sides(s):
        pq(1, s).wait_recv()
        pq(2, s).wait_recv()

    def corner(s):
        pq(3, s).wait_recv()
        gp(s + 1).wait_recv()

    partials(0)
    for s in range(NSUB):
        for q, r in BLOCKS:
            shapes_copy(q, r, s).start()
    parameters()
    partials(1, lambda: pass_on(0))
    partials(2, lambda: pass_on(1))
    kept_0 = local_states(0)
    partials(3, lambda: pass_on(2))
    finish(0, kept_0)
    kept_1 = local_states(1)
    pass_on(3)
    forward(0)
    finish(1, kept_1)
    kept_2 = local_states(2)
    share(0)
    gp(0).wait_recv()
    expand(0, 2, "first")
    forward(1)
    finish(2, kept_2)
    kept_3 = local_states(3)
    share_last(0)
    sides(0)
    expand(2, 4, "add")
    share(1)
    forward(2)
    finish(3, kept_3)
    share_last(1)
    corner(0)
    expand(6, 4, "add")
    sides(1)
    expand(10, 4, "add")
    share(2)
    forward(3)
    share_last(2)
    corner(1)
    expand(14, 4, "add")
    sides(2)
    expand(18, 4, "add")
    share(3)
    corner(2)
    expand(22, 4, "add")
    sides(3)
    expand(26, 4, "add")
    share_last(3)
    expand(30, 1, "add")
    pq(3, 3).wait_recv()
    expand(31, 1, "last")

    for s in range(NSUB):
        for q in range(4):
            core_copy(q, s).wait_send()
        for copy in (
            da(s), db(s), xa(s), xb(s), ya(s), yb(s), gxa(s), gxb(s), gya(s), gyb(s), gp(s), fa(s), fb(s),
            pq(1, s), pq(2, s), pq(3, s),
        ):
            copy.wait_send()
        for dk in range(1, tms):
            @pl.when(me + dk < tms)
            def _():
                state_copy(dk, s, me).wait_send()


def hand_over(*arrays):
    pieces = 4

    def copies(*refs):
        count = len(arrays)
        started = []
        for n in range(count):
            rows = arrays[n].shape[0] // pieces
            for piece in range(pieces):
                at = pl.ds(piece * rows, rows)
                started.append(
                    pltpu.make_async_copy(refs[n].at[at], refs[count + n].at[at], refs[2 * count].at[n, piece])
                )
        for copy in started:
            copy.start()
        for copy in started:
            copy.wait()

    return pl.pallas_call(
        copies,
        out_shape=tuple(jax.ShapeDtypeStruct(a.shape, a.dtype) for a in arrays),
        in_specs=[pl.BlockSpec(memory_space=pltpu.VMEM)] * len(arrays),
        out_specs=(pl.BlockSpec(memory_space=pltpu.HBM),) * len(arrays),
        scratch_shapes=[pltpu.SemaphoreType.DMA((len(arrays), pieces))],
        compiler_params=pltpu.CompilerParams(vmem_limit_bytes=16 * 1024 * 1024),
        cost_estimate=pl.CostEstimate(
            flops=0, bytes_accessed=sum(2 * a.size * a.dtype.itemsize for a in arrays), transcendentals=0
        ),
    )(*arrays)


def fused(tms, loads, phi, load_index, damping, frequency, gains, shapes):
    owned, steps, channels = damping.shape[0], loads.shape[0], loads.shape[1]
    rows, points, modes = phi.shape[0], shapes.shape[1], shapes.shape[0]
    width = owned // NSUB
    b16, f32 = jnp.bfloat16, jnp.float32
    packed = jnp.concatenate([damping, frequency, load_index.astype(f32), gains])
    kinds = TM + tms - 1
    small = pl.BlockSpec(memory_space=pltpu.VMEM)
    large = pl.BlockSpec(memory_space=pltpu.HBM)
    results = pl.pallas_call(
        functools.partial(kernel, tms),
        out_shape=(
            jax.ShapeDtypeStruct((steps, points), b16),
            jax.ShapeDtypeStruct((owned, steps), f32),
        ),
        in_specs=[small, small, large, large],
        out_specs=(small, small),
        scratch_shapes=[
            pltpu.VMEM((8, owned), f32),
            pltpu.VMEM((channels, rows), b16),
            pltpu.VMEM((steps, 128), f32),
            pltpu.VMEM((steps, rows), b16),
            pltpu.VMEM((NSUB, 4, 2, rows, width), b16),
            pltpu.VMEM((modes, points), b16),
            pltpu.VMEM((4, NSUB, steps, width), b16),
            pltpu.VMEM((4, NSUB, steps, width), b16),
            pltpu.VMEM((NSUB, 4, steps, width), f32),
        ] + [pltpu.VMEM((NSUB, steps, width), b16)] * 6 + [
            pltpu.VMEM((NSUB, width // 128, steps, 128), f32),
            pltpu.VMEM((NSUB, 8, width), f32),
            pltpu.VMEM((tms - 1, NSUB, 8, width), f32),
            pltpu.VMEM((NSUB, 8, width), f32),
            pltpu.VMEM((steps, modes), b16),
            pltpu.VMEM((steps, points), f32),
            pltpu.SemaphoreType.DMA((NSUB, kinds)),
            pltpu.SemaphoreType.DMA((NSUB, kinds)),
            pltpu.SemaphoreType.DMA((NSUB, 4, 2)),
            pltpu.SemaphoreType.DMA((NSUB, 4, 2)),
        ],
        compiler_params=pltpu.CompilerParams(
            collective_id=0, has_side_effects=True, vmem_limit_bytes=50 * 1024 * 1024
        ),
        cost_estimate=pl.CostEstimate(
            flops=2 * steps * (modes * (points + rows) + channels * rows),
            bytes_accessed=2 * (modes * points + rows * modes + steps * points),
            transcendentals=0,
        ),
    )(packed, loads, phi, shapes)
    return hand_over(*results)


def carried_in(value, axis, join, neutral):
    count, mine = (lax.axis_size(axis), lax.axis_index(axis))
    pieces = jax.tree.map(lambda part: lax.all_gather(part, axis), value)
    subtotal = jax.tree.map(
        lambda part, zero: jnp.full_like(part, 0) + jnp.asarray(zero, part.dtype), value, neutral
    )

    def step(position, subtotal):
        longer = join(subtotal, jax.tree.map(lambda part: part[position], pieces))
        return jax.tree.map(lambda new, old: jnp.where(position < mine, new, old), longer, subtotal)

    return lax.fori_loop(0, count - 1, step, subtotal)


def combine(earlier, later):
    ear, eai, ebr, ebi = earlier
    lar, lai, lbr, lbi = later
    return (
        lar * ear - lai * eai,
        lar * eai + lai * ear,
        lar * ebr - lai * ebi + lbr,
        lar * ebi + lai * ebr + lbi,
    )


def body(loads, phi, load_index, damping, frequency, gains, shapes):
    owned = damping.shape[0]
    steps = loads.shape[0]
    rows_here = phi.shape[0]
    local_index = load_index - lax.axis_index("dof") * rows_here
    selected = jnp.take(phi, local_index, axis=0)
    columns = lax.all_to_all(selected, "dof", split_axis=1, concat_axis=0, tiled=True)
    block = columns
    modal = lax.dot_general(
        block,
        lax.all_gather(loads, "dof", axis=1, tiled=True),
        (((0,), (1,)), ((), ())),
        preferred_element_type=jnp.float32,
    )
    drive = jnp.sqrt(-jnp.expm1(-2.0 * damping))
    width = min(128, steps)
    blocks = steps // width
    log_gain = jnp.cumsum(jnp.log(gains).reshape(blocks, width), axis=1)
    rise = jnp.exp(log_gain)
    fall = jnp.exp(-log_gain)
    offsets = jnp.arange(width, dtype=jnp.float32)
    lag = offsets[:, None] - offsets[None, :]
    lower = lag >= 0.0
    lag_pos = jnp.where(lower, lag, 0.0)
    decay = jnp.exp(-damping[:, None, None] * lag_pos[None, :, :])
    turn = frequency[:, None, None] * lag_pos[None, :, :]
    kernel_re = jnp.where(lower[None, :, :], decay * jnp.cos(turn), 0.0)
    kernel_im = jnp.where(lower[None, :, :], decay * jnp.sin(turn), 0.0)
    pushed = (drive[:, None] * modal).reshape(owned, blocks, width) * fall[None, :, :]
    local_re = (
        jnp.einsum("mts,mns->mnt", kernel_re, pushed, precision=lax.Precision.HIGHEST)
        * rise[None, :, :]
    )
    local_im = (
        jnp.einsum("mts,mns->mnt", kernel_im, pushed, precision=lax.Precision.HIGHEST)
        * rise[None, :, :]
    )
    ahead = offsets + 1.0
    power_mag = jnp.exp(-damping[:, None] * ahead[None, :])
    power_re = power_mag * jnp.cos(frequency[:, None] * ahead[None, :])
    power_im = power_mag * jnp.sin(frequency[:, None] * ahead[None, :])
    carry_re_all = power_re[:, None, :] * rise[None, :, :]
    carry_im_all = power_im[:, None, :] * rise[None, :, :]
    unit = jnp.ones((owned,), jnp.float32)
    nothing = jnp.zeros((owned,), jnp.float32)
    running = (unit, nothing, nothing, nothing)
    entering = []
    for index in range(blocks):
        entering.append(running)
        piece = (
            carry_re_all[:, index, width - 1],
            carry_im_all[:, index, width - 1],
            local_re[:, index, width - 1],
            local_im[:, index, width - 1],
        )
        running = combine(running, piece)
    incoming = carried_in(running, "tm", combine, (unit, nothing, nothing, nothing))
    state_re = []
    state_im = []
    for index in range(blocks):
        joined = combine(incoming, entering[index])
        state_re.append(joined[2])
        state_im.append(joined[3])
    enter_re = jnp.stack(state_re, axis=1)
    enter_im = jnp.stack(state_im, axis=1)
    history = (
        carry_re_all * enter_re[:, :, None] - carry_im_all * enter_im[:, :, None] + local_re
    ).reshape(owned, steps)
    rounded = history.astype(jnp.bfloat16)
    block = shapes
    field = lax.dot_general(
        lax.all_gather(rounded, "dof", axis=0, tiled=True),
        block,
        (((0,), (0,)), ((), ())),
        preferred_element_type=jnp.float32,
    )
    return (field.astype(jnp.bfloat16), history)


def solution(mesh):
    placed = (P("tm", "dof"), P("dof", None), P("dof"), P("dof"), P("dof"), P("tm"), P(None, "dof"))
    part = functools.partial(fused, mesh.shape["tm"]) if mesh.shape["dof"] == 8 else body
    return jax.shard_map(
        part,
        mesh=mesh,
        in_specs=placed,
        out_specs=(P("tm", "dof"), P("dof", "tm")),
        check_vma=False,
    )
```
